256 devices in a mesh: dp: 8 (over z), seq: 2 (over core), hid: 16 (over y, x).
Axes of the slice: x: 4, y: 4, z: 8, core: 2. Of those that a mesh axis runs over, the one named last changes fastest.
Arguments:
- tokens: bfloat16 [2, 4096, 4096], P(None, 'hid', ('dp', 'seq')), may hold values from -6 to 6
- cotangent: bfloat16 [2, 4096, 4096], P(None, 'hid', ('dp', 'seq')), may hold values from -6 to 6
- first_factors: bfloat16 [3, 3, 64, 64, 64], P(None, None, 'hid'), may hold values from -0.75 to 0.75
- second_factors: bfloat16 [3, 3, 64, 64, 64], P(None, None, 'hid'), may hold values from -0.75 to 0.75
- conv_taps: bfloat16 [3, 4, 4096], P(None, None, 'hid'), may hold values from -3 to 3
Outputs:
- input_grad: bfloat16 [2, 4096, 4096], P(None, 'hid', ('dp', 'seq'))
- first_grads: bfloat16 [3, 3, 64, 64, 64], P(None, None, 'hid')
- second_grads: bfloat16 [3, 3, 64, 64, 64], P(None, None, 'hid')
- tap_grads: bfloat16 [3, 4, 4096], P(None, None, 'hid')
The draws below stay inside these ranges and needn't reach their ends.
All inputs are finite; a program needn't handle non-finite values.
Results may differ from the reference program's by a relative error of at most 0.023.
Values may be sent and summed in bfloat16 or wider, within the bound.
A program may use at most 128 MiB of HBM per device.

```python
import math
import jax
import jax.numpy as jnp
from jax import lax

BLOCK = 64
D = 4096
TAPS = 4
LAYERS = 3
BATCH = 2
SEQ = 4096


def shard_levels(key, extent, split, low, top_value):
    gain = 1.0
    for axis_at, parts in split:
        heights = jax.random.uniform(jax.random.fold_in(jax.random.fold_in(key, 6), axis_at), (parts,), jnp.float32, low / len(split), top_value / len(split))
        gain = gain * jnp.repeat(jnp.exp(heights), extent[axis_at] // parts).reshape((-1,) + (1,) * (len(extent) - 1 - axis_at))
    return gain


def bell_draw(key, extent, scale, most, pieces=(), kind=jnp.bfloat16):
    array = jax.random.normal(key, extent, jnp.float32) * scale
    if len(pieces) > 0:
        array = shard_levels(key, extent, pieces, -0.22, 0.18) * array
    return jnp.clip(array, min=-most, max=most).astype(kind)


def setup_inputs(seed: int = 0) -> dict:
    keys = jax.random.split(jax.random.key(seed), 6)
    return {
        "tokens": bell_draw(keys[0], (BATCH, D, SEQ), 1.0, 6.0, ((1, 16), (2, 16))),
        "cotangent": bell_draw(keys[1], (BATCH, D, SEQ), 1.0, 6.0, ((1, 16), (2, 16))),
        "first_factors": bell_draw(keys[2], (LAYERS, 3, BLOCK, BLOCK, BLOCK), BLOCK ** -0.5, 0.75, ((2, 16),)),
        "second_factors": bell_draw(keys[3], (LAYERS, 3, BLOCK, BLOCK, BLOCK), BLOCK ** -0.5, 0.75, ((2, 16),)),
        "conv_taps": bell_draw(keys[4], (LAYERS, TAPS, D), 0.5, 3.0, ((2, 16),)),
    }


def section_one(inputs, first):
    return jnp.einsum('abs,mabj->majs', inputs.astype(jnp.float32), first.astype(jnp.float32)).astype(jnp.bfloat16)

def section_two(grouped, second):
    return jnp.einsum('majs,mjak->mjks', grouped.astype(jnp.float32), second.astype(jnp.float32))

def monarch_back(inputs, grouped, upstream, first, second):
    upper = upstream.astype(jnp.float32)
    second_grad = jnp.einsum('majs,mjks->mjak', grouped.astype(jnp.float32), upper)
    spread = jnp.einsum('mjks,mjak->mjas', upper, second.astype(jnp.float32)).astype(jnp.bfloat16)
    spread_wide = spread.astype(jnp.float32)
    first_grad = jnp.einsum('abs,mjas->mabj', inputs.astype(jnp.float32), spread_wide)
    input_back = jnp.einsum('mjas,mabj->abs', spread_wide, first.astype(jnp.float32))
    return (first_grad, second_grad, input_back)

def reference(tokens, cotangent, first_factors, second_factors, conv_taps):
    rim_width = TAPS - 1
    scale_back = 1.0 / math.sqrt(BATCH * SEQ)
    first_total = jnp.zeros(first_factors.shape, jnp.float32)
    second_total = jnp.zeros(second_factors.shape, jnp.float32)
    taps_total = jnp.zeros(conv_taps.shape, jnp.float32)
    results = []
    for member in range(BATCH):
        stream = tokens[member]
        stored = []
        for depth in range(LAYERS):
            inputs = stream.reshape(BLOCK, BLOCK, SEQ)
            grouped = section_one(inputs, first_factors[depth, 0:2])
            projected = section_two(grouped, second_factors[depth, 0:2]).astype(jnp.bfloat16)
            queries = projected[0].reshape(D, SEQ)
            signal = projected[1].reshape(D, SEQ)
            padded = jnp.concatenate((jnp.zeros((D, rim_width), jnp.bfloat16), signal), axis=1).astype(jnp.float32)
            kernel = conv_taps[depth].astype(jnp.float32)
            convolved = jnp.zeros((D, SEQ), jnp.float32)
            for offset in range(rim_width + 1):
                convolved = convolved + kernel[offset][:, None] * padded[:, rim_width - offset:rim_width - offset + SEQ]
            opened = jax.nn.sigmoid(queries.astype(jnp.float32))
            gated_rows = (opened * convolved).astype(jnp.bfloat16)
            gated_blocks = gated_rows.reshape(BLOCK, BLOCK, SEQ)
            out_grouped = section_one(gated_blocks, first_factors[depth, 2:3])
            branch = section_two(out_grouped, second_factors[depth, 2:3])
            stream = (stream.astype(jnp.float32) + branch.reshape(D, SEQ)).astype(jnp.bfloat16)
            stored.append((inputs, grouped, padded, opened, convolved, gated_blocks, out_grouped))
        flowing = cotangent[member].astype(jnp.float32)
        for depth in reversed(range(LAYERS)):
            inputs, grouped, padded, opened, convolved, gated_blocks, out_grouped = stored[depth]
            upstream = flowing.astype(jnp.bfloat16).reshape(1, BLOCK, BLOCK, SEQ)
            out_first, out_second, gated_back = monarch_back(gated_blocks, out_grouped, upstream, first_factors[depth, 2:3], second_factors[depth, 2:3])
            gated_back = gated_back.reshape(D, SEQ)
            conv_back = gated_back * opened
            query_back = gated_back * convolved * opened * (1.0 - opened)
            extended = jnp.concatenate((conv_back, jnp.zeros((D, rim_width), jnp.float32)), axis=1)
            kernel = conv_taps[depth].astype(jnp.float32)
            signal_back = jnp.zeros((D, SEQ), jnp.float32)
            tap_rows = []
            for offset in range(rim_width + 1):
                signal_back = signal_back + kernel[offset][:, None] * extended[:, offset:offset + SEQ]
                tap_rows.append(lax.optimization_barrier(jnp.sum(conv_back * padded[:, rim_width - offset:rim_width - offset + SEQ], axis=1)))
            pair_back = jnp.stack((query_back, signal_back)).astype(jnp.bfloat16).reshape(2, BLOCK, BLOCK, SEQ)
            in_first, in_second, input_back = monarch_back(inputs, grouped, pair_back, first_factors[depth, 0:2], second_factors[depth, 0:2])
            flowing = flowing + input_back.reshape(D, SEQ)
            first_total = first_total.at[depth].add(jnp.concatenate((in_first, out_first), axis=0))
            second_total = second_total.at[depth].add(jnp.concatenate((in_second, out_second), axis=0))
            taps_total = taps_total.at[depth].add(jnp.stack(tap_rows))
        results.append(flowing.astype(jnp.bfloat16))
    input_grad = jnp.stack(results)
    first_grads = (first_total * scale_back).astype(jnp.bfloat16)
    second_grads = (second_total * scale_back).astype(jnp.bfloat16)
    tap_grads = (taps_total * scale_back).astype(jnp.bfloat16)
    return (input_grad, first_grads, second_grads, tap_grads)
```

```python
import functools
import math

import jax
import jax.numpy as jnp
from jax import lax
from jax.experimental import pallas as pl
from jax.experimental.pallas import tpu as pltpu
from jax.sharding import PartitionSpec as P

MESH = pl.DeviceIdType.MESH
BF = jnp.bfloat16
F32 = jnp.float32
LANES = 128
ROWS = 32


def iota(shape, dim):
    return lax.broadcasted_iota(jnp.int32, shape, dim)


def nn(a, b):
    return lax.dot_general(a, b, (((1,), (0,)), ((), ())), preferred_element_type=F32)


def nt(a, b):
    return lax.dot_general(a, b, (((1,), (1,)), ((), ())), preferred_element_type=F32)


def ones_where(condition):
    return jnp.where(condition, 1.0, 0.0).astype(BF)


def kernel(
    dims,
    tok,
    cot,
    first,
    second,
    taps,
    out_x,
    out_first,
    out_second,
    out_taps,
    c_exp1,
    c_exp2,
    c_mask1,
    c_mask1t,
    c_mask2,
    c_mask2t,
    c_perm,
    c_permt,
    c_pack1,
    c_pack2,
    w_p,
    w_pt,
    w_qf,
    w_qb,
    w_taps,
    xs,
    us,
    gs,
    opened,
    convolved,
    upo,
    upq,
    flow,
    cb,
    s_q,
    r_q,
    s_o,
    r_o,
    z_o,
    t_o,
    z_q,
    t_q,
    h_fs,
    h_fr,
    h_bs,
    h_br,
    tap_acc,
    g_out,
    g_in,
    g_sum,
    tp_out,
    tp_in,
    tap_total,
    reg_send,
    reg_recv,
    edge_send,
    edge_recv,
    sum_send,
    sum_recv,
):
    layers, ntaps, batch, chan, width, nb, nh, nz, ns = dims
    nx = int(math.isqrt(nh))
    ny = nh // nx
    parts = nz * ns
    block = chan // nh
    share = chan // parts
    pair = 2 * nb
    scale = 1.0 / math.sqrt(batch * parts * width)

    me_h = lax.axis_index("hid")
    me_y, me_x = me_h // nx, me_h % nx
    me_p = lax.axis_index("dp") * ns + lax.axis_index("seq")

    def hid_peer(k):
        return ((me_y + k // nx) % ny) * nx + (me_x + k % nx) % nx

    def part_at(p):
        return {"dp": p // ns, "seq": p % ns}

    def part_peer(k):
        return (me_p + k) % parts

    barrier = pltpu.get_barrier_semaphore()

    def greet_hid(k, _):
        pl.semaphore_signal(barrier, inc=1, device_id={"hid": hid_peer(k)}, device_id_type=MESH)
        return 0

    def greet_part(k, _):
        pl.semaphore_signal(
            barrier, inc=1, device_id=part_at(part_peer(k)), device_id_type=MESH
        )
        return 0

    lax.fori_loop(1, nh, greet_hid, 0)
    lax.fori_loop(1, parts, greet_part, 0)

    lb_shift = 2
    nb_shift = nb.bit_length() - 1
    r_c = iota((chan, nb), 0)
    k_c = iota((chan, nb), 1)
    c_exp1[...] = ones_where(k_c == ((r_c >> 4) << lb_shift) + (r_c & 3))
    c_exp2[...] = ones_where(k_c == (r_c & (nb - 1)))
    r_s = iota((chan, chan), 0)
    c_s = iota((chan, chan), 1)
    c_mask1[...] = ones_where(((c_s >> 2) & 3) == (r_s >> nb_shift))
    c_mask1t[...] = ones_where(((r_s >> 2) & 3) == (c_s >> nb_shift))
    c_mask2[...] = ones_where((r_s & 3) == (c_s >> nb_shift))
    c_mask2t[...] = ones_where((c_s & 3) == (r_s >> nb_shift))
    c_perm[...] = ones_where(c_s == ((r_s & 3) << nb_shift) + (r_s >> 2))
    c_permt[...] = ones_where(r_s == ((c_s & 3) << nb_shift) + (c_s >> 2))
    r_p = iota((chan, pair), 0)
    k_p = iota((chan, pair), 1)
    c_pack1[...] = ones_where(k_p == ((r_p >> 4) << lb_shift) + (r_p & 3))
    c_pack2[...] = ones_where(k_p == nb + (r_p & (nb - 1)))

    def make_pt(i):
        w_pt[i] = nt(c_exp1[...], first[i]).astype(BF) * c_mask1t[...]

    def make_p(i):
        w_p[i] = nt(first[i], c_exp1[...]).astype(BF) * c_mask1[...]

    def make_q(i):
        rows = nn(c_perm[...], second[i]).astype(BF)
        w_qb[i] = nt(rows, c_exp2[...]).astype(BF) * c_mask2[...]
        w_qf[i] = nt(c_exp2[...], rows).astype(BF) * c_mask2t[...]

    def make_taps(layer):
        same = ones_where(iota((chan, chan), 0) == iota((chan, chan), 1))
        columns = nt(same, taps[layer]).astype(BF)
        lane = iota((ntaps, ntaps * LANES), 1) >> 7
        spread = ones_where(lane == iota((ntaps, ntaps * LANES), 0))
        w_taps[layer] = nn(columns, spread)

    def regroup_sem(kind, layer, b):
        return (kind * layers + layer) * batch + b

    def regroup_start(source, target, kind, layer, b):
        sem = regroup_sem(kind, layer, b)
        own = pl.ds(pl.multiple_of(me_h * block, block), block)
        target[layer, b, own, :] = source[layer, b, own, :]

        def send(k, _):
            peer = hid_peer(k)
            pltpu.make_async_remote_copy(
                src_ref=source.at[layer, b, pl.ds(pl.multiple_of(peer * block, block), block)],
                dst_ref=target.at[layer, b, own],
                send_sem=reg_send.at[sem],
                recv_sem=reg_recv.at[sem],
                device_id={"hid": peer},
                device_id_type=MESH,
            ).start()
            return 0

        lax.fori_loop(1, nh, send, 0)

    def regroup_copy(source, target, kind, layer, b):
        sem = regroup_sem(kind, layer, b)
        rest = pl.ds(0, (nh - 1) * block)
        return pltpu.make_async_remote_copy(
            src_ref=source.at[layer, b, rest],
            dst_ref=target.at[layer, b, rest],
            send_sem=reg_send.at[sem],
            recv_sem=reg_recv.at[sem],
            device_id={"hid": hid_peer(1)},
            device_id_type=MESH,
        )

    def edge_copy(source, target, kind, layer, b, step):
        sem = (kind * layers + layer) * batch + b
        return pltpu.make_async_remote_copy(
            src_ref=source.at[layer, b],
            dst_ref=target.at[layer, b],
            send_sem=edge_send.at[sem],
            recv_sem=edge_recv.at[sem],
            device_id=part_at((me_p + step + parts) % parts),
            device_id_type=MESH,
        )

    def scatter_start(source, target, sem, layer):
        own = pl.ds(pl.multiple_of(me_p * share, share), share)
        target[layer, own, :] = source[layer, own, :]

        def send(k, _):
            peer = part_peer(k)
            pltpu.make_async_remote_copy(
                src_ref=source.at[layer, pl.ds(pl.multiple_of(peer * share, share), share)],
                dst_ref=target.at[layer, own],
                send_sem=sum_send.at[sem],
                recv_sem=sum_recv.at[sem],
                device_id=part_at(peer),
                device_id_type=MESH,
            ).start()
            return 0

        lax.fori_loop(1, parts, send, 0)

    def gather_start(target, sem, layer):
        own = pl.ds(pl.multiple_of(me_p * share, share), share)

        def send(k, _):
            pltpu.make_async_remote_copy(
                src_ref=target.at[layer, own],
                dst_ref=target.at[layer, own],
                send_sem=sum_send.at[sem],
                recv_sem=sum_recv.at[sem],
                device_id=part_at(part_peer(k)),
                device_id_type=MESH,
            ).start()
            return 0

        lax.fori_loop(1, parts, send, 0)

    def sum_copy(source, target, sem, layer):
        rest = pl.ds(0, (parts - 1) * share)
        return pltpu.make_async_remote_copy(
            src_ref=source.at[layer, rest],
            dst_ref=target.at[layer, rest],
            send_sem=sum_send.at[sem],
            recv_sem=sum_recv.at[sem],
            device_id=part_at(part_peer(1)),
            device_id_type=MESH,
        )

    def taps_start():
        own = pl.ds(pl.multiple_of(me_p * 16, 16), 16)

        def send(k, _):
            pltpu.make_async_remote_copy(
                src_ref=tp_out,
                dst_ref=tp_in.at[own],
                send_sem=sum_send.at[2 * layers],
                recv_sem=sum_recv.at[2 * layers],
                device_id=part_at(part_peer(k)),
                device_id_type=MESH,
            ).start()
            return 0

        tp_in[own, :] = tp_out[...]
        lax.fori_loop(1, parts, send, 0)

    def taps_copy():
        rest = pl.ds(0, (parts - 1) * 16)
        return pltpu.make_async_remote_copy(
            src_ref=tp_in.at[rest],
            dst_ref=tp_in.at[rest],
            send_sem=sum_send.at[2 * layers],
            recv_sem=sum_recv.at[2 * layers],
            device_id=part_at(part_peer(1)),
            device_id_type=MESH,
        )

    def in_rows(step):
        def one(r, _):
            step(pl.ds(pl.multiple_of(r * ROWS, ROWS), ROWS))
            return 0

        lax.fori_loop(0, chan // ROWS, one, 0)

    has_before = jnp.where(me_p > 0, 1.0, 0.0).astype(F32)
    has_after = jnp.where(me_p < parts - 1, 1.0, 0.0).astype(F32)

    def f1(b, layer):
        x = xs[layer, b]
        s_q[layer, b, :, :width] = nn(w_pt[3 * layer], x).astype(BF)
        s_q[layer, b, :, width:] = nn(w_pt[3 * layer + 1], x).astype(BF)
        regroup_start(s_q, r_q, 0, layer, b)

    def f2(b, layer):
        regroup_copy(s_q, r_q, 0, layer, b).wait_recv()
        signal = nn(w_qf[3 * layer + 1], r_q[layer, b, :, width:]).astype(BF)
        us[layer, b] = signal
        h_fs[layer, b] = signal[:, width - LANES :]
        edge_copy(h_fs, h_fr, 0, layer, b, 1).start()
        query = nn(w_qf[3 * layer], r_q[layer, b, :, :width]).astype(BF).astype(F32)
        opened[layer, b] = jax.nn.sigmoid(query)

    def f3(b, layer):
        edge_copy(h_fs, h_fr, 0, layer, b, 1).wait_recv()

        def step(rows):
            before = h_fr[layer, b, rows, :].astype(F32) * has_before
            signal = us[layer, b, rows, :].astype(F32)
            extended = jnp.concatenate((before, signal), axis=1)
            total = jnp.zeros((ROWS, width), F32)
            for i in range(ntaps):
                tap = w_taps[layer, rows, i * LANES : (i + 1) * LANES]
                tap = jnp.concatenate([tap] * (width // LANES), axis=1)
                moved = signal if i == 0 else pltpu.roll(extended, i, 1)[:, LANES:]
                total = total + tap * moved
            convolved[layer, b, rows, :] = total
            gs[layer, b, rows, :] = (opened[layer, b, rows, :] * total).astype(BF)

        in_rows(step)
        s_o[layer, b] = nn(w_pt[3 * layer + 2], gs[layer, b]).astype(BF)
        regroup_start(s_o, r_o, 1, layer, b)

    def f4(b, layer):
        regroup_copy(s_o, r_o, 1, layer, b).wait_recv()
        if layer + 1 < layers:
            branch = nn(w_qf[3 * layer + 2], r_o[layer, b])
            xs[layer + 1, b] = (xs[layer, b].astype(F32) + branch).astype(BF)

    def b1(b, layer):
        if layer == layers - 1:
            upstream = cot[b]
        else:
            upstream = flow[b].astype(BF)
        upo[layer, b] = upstream
        z_o[layer, b] = nn(w_qb[3 * layer + 2], upstream).astype(BF)
        regroup_start(z_o, t_o, 2, layer, b)

    def b2(b, layer):
        regroup_copy(z_o, t_o, 2, layer, b).wait_recv()
        cb[b] = nn(w_p[3 * layer + 2], t_o[layer, b])

        def step(rows):
            back = cb[b, rows, :]
            gate = opened[layer, b, rows, :]
            conv_back = back * gate
            cb[b, rows, :] = conv_back
            h_bs[layer, b, rows, :] = conv_back[:, :LANES].astype(BF)
            upq[layer, b, rows, :width] = (
                conv_back * convolved[layer, b, rows, :] * (1.0 - gate)
            ).astype(BF)

        in_rows(step)
        edge_copy(h_bs, h_br, 1, layer, b, -1).start()

    def b3(b, layer):
        edge_copy(h_bs, h_br, 1, layer, b, -1).wait_recv()

        def step(rows):
            after = h_br[layer, b, rows, :].astype(F32) * has_after
            conv_back = cb[b, rows, :]
            extended = jnp.concatenate((conv_back, after), axis=1)
            signal = us[layer, b, rows, :].astype(F32)
            total = jnp.zeros((ROWS, width), F32)
            for i in range(ntaps):
                tap = w_taps[layer, rows, i * LANES : (i + 1) * LANES]
                tap = jnp.concatenate([tap] * (width // LANES), axis=1)
                if i == 0:
                    moved = conv_back
                else:
                    moved = pltpu.roll(extended, width + LANES - i, 1)[:, :width]
                total = total + tap * moved
                term = moved * signal
                narrow = term[:, :LANES]
                for q in range(1, width // LANES):
                    narrow = narrow + term[:, q * LANES : (q + 1) * LANES]
                lanes = slice(i * LANES, (i + 1) * LANES)
                if b > 0:
                    narrow = narrow + tap_acc[rows, lanes]
                tap_acc[rows, lanes] = narrow
            upq[layer, b, rows, width:] = total.astype(BF)

        in_rows(step)
        z_q[layer, b, :, :width] = nn(w_qb[3 * layer], upq[layer, b, :, :width]).astype(BF)
        z_q[layer, b, :, width:] = nn(w_qb[3 * layer + 1], upq[layer, b, :, width:]).astype(BF)
        regroup_start(z_q, t_q, 3, layer, b)

    def b4(b, layer):
        regroup_copy(z_q, t_q, 3, layer, b).wait_recv()
        back = nn(w_p[3 * layer], t_q[layer, b, :, :width]) + nn(
            w_p[3 * layer + 1], t_q[layer, b, :, width:]
        )
        before = cot[b].astype(F32) if layer == layers - 1 else flow[b]
        if layer > 0:
            flow[b] = before + back
        else:
            out_x[b] = (before + back).astype(BF)

    def tap_rows(layer):
        total = jnp.zeros((16, chan), F32)
        for i in range(ntaps):
            part = tap_acc[:, i * LANES : (i + 1) * LANES]
            high = part.astype(BF)
            low = (part - high.astype(F32)).astype(BF)
            row = ones_where(iota((16, LANES), 0) == layer * ntaps + i)
            total = total + nt(row, high) + nt(row, low)
        if layer == layers - 1:
            tap_total[...] = total
        else:
            tap_total[...] += total

    def grads(layer, m, inputs, spread, sections, upstream):
        one = nt(inputs[0], spread[0])
        two = nt(sections[0], upstream[0])
        for b in range(1, batch):
            one = one + nt(inputs[b], spread[b])
            two = two + nt(sections[b], upstream[b])
        packed = nn(one.astype(BF) * c_mask1[...], c_pack1[...])
        other = nn(two.astype(BF) * c_mask2[...], c_pack2[...]).astype(BF)
        packed = packed + nn(c_permt[...], other)
        g_out[layer, :, m * pair : (m + 1) * pair] = packed.astype(BF)

    both = range(batch)

    def grads_o(layer):
        grads(
            layer,
            2,
            [gs[layer, b] for b in both],
            [t_o[layer, b] for b in both],
            [r_o[layer, b] for b in both],
            [upo[layer, b] for b in both],
        )

    def grads_in(layer):
        for m in range(2):
            lanes = slice(m * width, (m + 1) * width)
            grads(
                layer,
                m,
                [xs[layer, b] for b in both],
                [t_q[layer, b, :, lanes] for b in both],
                [r_q[layer, b, :, lanes] for b in both],
                [upq[layer, b, :, lanes] for b in both],
            )
        scatter_start(g_out, g_in, layer, layer)

    def total_up(layer):
        sum_copy(g_out, g_in, layer, layer).wait_recv()
        total = g_in[layer, :share, :].astype(F32)
        for p in range(1, parts):
            total = total + g_in[layer, p * share : (p + 1) * share, :].astype(F32)
        own = pl.ds(pl.multiple_of(me_p * share, share), share)
        g_sum[layer, own, :] = (total * scale).astype(BF)
        gather_start(g_sum, layers + layer, layer)

    def finish(layer):
        sum_copy(g_sum, g_sum, layers + layer, layer).wait_recv()
        for m in range(3):
            out_first[3 * layer + m] = g_sum[layer, :, m * pair : m * pair + nb]
            out_second[3 * layer + m] = g_sum[layer, :, m * pair + nb : (m + 1) * pair]

    for b in both:
        xs[0, b] = tok[b]
    make_pt(0)
    make_pt(1)
    pl.semaphore_wait(barrier, nh - 1 + parts - 1)
    for b in both:
        f1(b, 0)
    for i in range(3):
        make_q(i)
    make_pt(2)
    make_taps(0)
    for layer in range(layers):
        for b in both:
            f2(b, layer)
        if layer + 1 < layers:
            for m in range(3):
                make_q(3 * layer + 3 + m)
                make_pt(3 * layer + 3 + m)
            make_taps(layer + 1)
        for b in both:
            f3(b, layer)
        for m in range(3):
            make_p(3 * layer + m)
        if layer == layers - 1:
            for b in both:
                b1(b, layer)
        for b in both:
            f4(b, layer)
            if layer + 1 < layers:
                f1(b, layer + 1)
    for layer in reversed(range(layers)):
        for b in both:
            b2(b, layer)
        for b in both:
            b3(b, layer)
        tap_rows(layer)
        grads_o(layer)
        if layer == 0:
            tp_out[...] = tap_total[...].astype(BF)
            taps_start()
        if layer + 1 < layers:
            total_up(layer + 1)
        for b in both:
            b4(b, layer)
            if layer > 0:
                b1(b, layer - 1)
        grads_in(layer)
        if layer + 1 < layers:
            finish(layer + 1)
    taps_copy().wait_recv()
    total = tp_in[:16, :].astype(F32)
    for p in range(1, parts):
        total = total + tp_in[p * 16 : (p + 1) * 16, :].astype(F32)
    total = (total * scale).astype(BF)
    for layer in range(layers):
        out_taps[layer] = total[layer * ntaps : (layer + 1) * ntaps, :]
    total_up(0)
    finish(0)

    for layer in range(layers):
        for b in both:
            regroup_copy(s_q, r_q, 0, layer, b).wait_send()
            regroup_copy(s_o, r_o, 1, layer, b).wait_send()
            regroup_copy(z_o, t_o, 2, layer, b).wait_send()
            regroup_copy(z_q, t_q, 3, layer, b).wait_send()
            edge_copy(h_fs, h_fr, 0, layer, b, 1).wait_send()
            edge_copy(h_bs, h_br, 1, layer, b, -1).wait_send()
        sum_copy(g_out, g_in, layer, layer).wait_send()
        sum_copy(g_sum, g_sum, layers + layer, layer).wait_send()
    taps_copy().wait_send()


def body(sizes, tokens, cotangent, first_factors, second_factors, conv_taps):
    nh, nz, ns = sizes
    batch, chan, width = tokens.shape
    layers, ntaps, _ = conv_taps.shape
    nb = first_factors.shape[3]
    projections = first_factors.shape[1]
    parts = nz * ns
    share = chan // parts
    pair = 2 * nb
    many = layers * projections
    dims = (layers, ntaps, batch, chan, width, nb, nh, nz, ns)
    V = pltpu.VMEM
    sq = (chan, chan)
    act = (layers, batch, chan, width)
    wide = (layers, batch, chan, 2 * width)
    edge = (layers, batch, chan, LANES)
    grad = (layers, chan, projections * pair)
    scratch = [
        V((chan, nb), BF),
        V((chan, nb), BF),
        V(sq, BF),
        V(sq, BF),
        V(sq, BF),
        V(sq, BF),
        V(sq, BF),
        V(sq, BF),
        V((chan, pair), BF),
        V((chan, pair), BF),
        V((many,) + sq, BF),
        V((many,) + sq, BF),
        V((many,) + sq, BF),
        V((many,) + sq, BF),
        V((layers, chan, ntaps * LANES), F32),
        V(act, BF),
        V(act, BF),
        V(act, BF),
        V(act, F32),
        V(act, F32),
        V(act, BF),
        V(wide, BF),
        V((batch, chan, width), F32),
        V((batch, chan, width), F32),
        V(wide, BF),
        V(wide, BF),
        V(act, BF),
        V(act, BF),
        V(act, BF),
        V(act, BF),
        V(wide, BF),
        V(wide, BF),
        V(edge, BF),
        V(edge, BF),
        V(edge, BF),
        V(edge, BF),
        V((chan, ntaps * LANES), F32),
        V(grad, BF),
        V((layers, parts * share, projections * pair), BF),
        V(grad, BF),
        V((16, chan), BF),
        V((parts * 16, chan), BF),
        V((16, chan), F32),
        pltpu.SemaphoreType.DMA((4 * layers * batch,)),
        pltpu.SemaphoreType.DMA((4 * layers * batch,)),
        pltpu.SemaphoreType.DMA((2 * layers * batch,)),
        pltpu.SemaphoreType.DMA((2 * layers * batch,)),
        pltpu.SemaphoreType.DMA((2 * layers + 1,)),
        pltpu.SemaphoreType.DMA((2 * layers + 1,)),
    ]
    whole = pl.BlockSpec(memory_space=pltpu.VMEM)
    out_x, out_first, out_second, out_taps = pl.pallas_call(
        functools.partial(kernel, dims),
        out_shape=(
            jax.ShapeDtypeStruct((batch, chan, width), BF),
            jax.ShapeDtypeStruct((many, chan, nb), BF),
            jax.ShapeDtypeStruct((many, chan, nb), BF),
            jax.ShapeDtypeStruct((layers, ntaps, chan), BF),
        ),
        in_specs=[whole] * 5,
        out_specs=[whole] * 4,
        scratch_shapes=scratch,
        compiler_params=pltpu.CompilerParams(
            collective_id=0, has_side_effects=True, vmem_limit_bytes=56 * 1024 * 1024
        ),
    )(
        tokens,
        cotangent,
        first_factors.reshape(many, chan, nb),
        second_factors.reshape(many, chan, nb),
        conv_taps,
    )
    return (
        out_x,
        out_first.reshape(first_factors.shape),
        out_second.reshape(second_factors.shape),
        out_taps,
    )


def solution(mesh):
    sizes = (mesh.shape["hid"], mesh.shape["dp"], mesh.shape["seq"])
    return jax.shard_map(
        functools.partial(body, sizes),
        mesh=mesh,
        in_specs=(
            P(None, "hid", ("dp", "seq")),
            P(None, "hid", ("dp", "seq")),
            P(None, None, "hid", None, None),
            P(None, None, "hid", None, None),
            P(None, None, "hid"),
        ),
        out_specs=(
            P(None, "hid", ("dp", "seq")),
            P(None, None, "hid", None, None),
            P(None, None, "hid", None, None),
            P(None, None, "hid"),
        ),
        check_vma=False,
    )
```

```python
import functools
import math

import jax
import jax.numpy as jnp
from jax import lax
from jax.experimental import pallas as pl
from jax.experimental.pallas import tpu as pltpu
from jax.sharding import PartitionSpec as P

MESH = pl.DeviceIdType.MESH
BF = jnp.bfloat16
F32 = jnp.float32
LANES = 128
ROWS = 32


def iota(shape, dim):
    return lax.broadcasted_iota(jnp.int32, shape, dim)


def nn(a, b):
    return lax.dot_general(a, b, (((1,), (0,)), ((), ())), preferred_element_type=F32)


def nt(a, b):
    return lax.dot_general(a, b, (((1,), (1,)), ((), ())), preferred_element_type=F32)


def ones_where(condition):
    return jnp.where(condition, 1.0, 0.0).astype(BF)


def kernel(
    dims,
    tok,
    cot,
    first,
    second,
    taps,
    out_x,
    g_sum,
    out_taps,
    c_exp1,
    c_exp2,
    c_mask1,
    c_mask1t,
    c_mask2,
    c_mask2t,
    c_perm,
    c_permt,
    c_pack1,
    c_pack2,
    c_same,
    w_p,
    w_pt,
    w_qf,
    w_qb,
    w_taps,
    xs,
    us,
    gs,
    opened,
    convolved,
    ups,
    flow,
    cb,
    sent,
    got,
    edge_out,
    edge_in,
    edge_wide,
    tap_acc,
    g_out,
    g_in,
    tp_out,
    tp_in,
    tap_total,
    reg_send,
    reg_recv,
    edge_send,
    edge_recv,
    sum_send,
    sum_recv,
):
    layers, ntaps, batch, chan, width, nb, nh, nz, ns = dims
    nx = int(math.isqrt(nh))
    ny = nh // nx
    parts = nz * ns
    block = chan // nh
    share = chan // parts
    pair = 2 * nb
    scale = 1.0 / math.sqrt(batch * parts * width)

    me_h = lax.axis_index("hid")
    me_y, me_x = me_h // nx, me_h % nx
    me_z, me_c = lax.axis_index("dp"), lax.axis_index("seq")
    me_p = me_z * ns + me_c

    def far(k, n):
        return min(k, n - k)

    def hid_at(h):
        return (me_z, me_c, h)

    def part_at(p):
        return (p // ns, p % ns, me_h)

    turns = [(dy, dx) for dy in range(ny) for dx in range(nx) if dy + dx > 0]
    turns.sort(key=lambda t: -far(t[0], ny) - far(t[1], nx))
    peers_y = [(me_y + dy) % ny * nx for dy in range(ny)]
    peers_x = [(me_x + dx) % nx for dx in range(nx)]
    hid_peers = [peers_y[dy] + peers_x[dx] for dy, dx in turns]
    steps = sorted(range(1, parts), key=lambda k: -far(k, parts))
    part_peers = [(me_p + k) % parts for k in steps]
    part_ids = [part_at(p) for p in part_peers]

    barrier = pltpu.get_barrier_semaphore()

    for h in hid_peers:
        pl.semaphore_signal(barrier, inc=1, device_id=hid_at(h), device_id_type=MESH)
    for where in part_ids:
        pl.semaphore_signal(barrier, inc=1, device_id=where, device_id_type=MESH)

    nb_shift = nb.bit_length() - 1
    r_c, k_c = iota((chan, nb), 0), iota((chan, nb), 1)
    r_s, c_s = iota((chan, chan), 0), iota((chan, chan), 1)
    r_p, k_p = iota((chan, pair), 0), iota((chan, pair), 1)

    def constants_first():
        c_exp1[...] = ones_where(k_c == ((r_c >> 4) << 2) + (r_c & 3))
        c_mask1t[...] = ones_where(((r_s >> 2) & 3) == (c_s >> nb_shift))

    def constants_second():
        c_exp2[...] = ones_where(k_c == (r_c & (nb - 1)))
        c_perm[...] = ones_where(c_s == ((r_s & 3) << nb_shift) + (r_s >> 2))
        c_mask2[...] = ones_where((r_s & 3) == (c_s >> nb_shift))
        c_mask2t[...] = ones_where((c_s & 3) == (r_s >> nb_shift))
        c_same[...] = ones_where(r_s == c_s)

    def constants_last():
        c_mask1[...] = ones_where(((c_s >> 2) & 3) == (r_s >> nb_shift))
        c_permt[...] = ones_where(r_s == ((c_s & 3) << nb_shift) + (c_s >> 2))
        for half in range(2):
            to1 = half * nb + ((r_p >> 4) << 2) + (r_p & 3)
            c_pack1[half] = ones_where(k_p == to1)
            c_pack2[half] = ones_where(k_p == half * nb + (r_p & (nb - 1)))

    def make_pt(i):
        w_pt[i] = nt(c_exp1[...], first[i]).astype(BF) * c_mask1t[...]

    def make_p(i):
        w_p[i] = nt(first[i], c_exp1[...]).astype(BF) * c_mask1[...]

    def make_q(i):
        rows = nn(c_perm[...], second[i]).astype(BF)
        w_qb[i] = nt(rows, c_exp2[...]).astype(BF) * c_mask2[...]
        w_qf[i] = nt(c_exp2[...], rows).astype(BF) * c_mask2t[...]

    def make_taps(layer):
        columns = nt(c_same[...], taps[layer]).astype(BF)
        lane = iota((ntaps, ntaps * LANES), 1) >> 7
        spread = ones_where(lane == iota((ntaps, ntaps * LANES), 0))
        w_taps[layer] = nn(columns, spread)

    own_rows = pl.ds(pl.multiple_of(me_h * block, block), block)

    def at(kind, layer, b):
        return (kind * layers + layer) * batch + b

    def regroup_start(i):
        got[i, own_rows, :] = sent[i, own_rows, :]

        for peer in hid_peers:
            pltpu.make_async_remote_copy(
                src_ref=sent.at[i, pl.ds(pl.multiple_of(peer * block, block), block)],
                dst_ref=got.at[i, own_rows],
                send_sem=reg_send.at[i],
                recv_sem=reg_recv.at[i],
                device_id=hid_at(peer),
                device_id_type=MESH,
            ).start()

    def regroup_copy(i):
        rest = pl.ds(0, (nh - 1) * block)
        return pltpu.make_async_remote_copy(
            src_ref=sent.at[i, rest],
            dst_ref=got.at[i, rest],
            send_sem=reg_send.at[i],
            recv_sem=reg_recv.at[i],
            device_id=hid_at(hid_peers[0]),
            device_id_type=MESH,
        )

    edge = ntaps - 1

    def edge_copy(kind, layer, b):
        i = at(kind, layer, b)
        step = steps.index(1 if kind == 0 else parts - 1)
        return pltpu.make_async_remote_copy(
            src_ref=edge_out.at[i],
            dst_ref=edge_in.at[i],
            send_sem=edge_send.at[i],
            recv_sem=edge_recv.at[i],
            device_id=part_ids[step],
            device_id_type=MESH,
        )

    e_r, e_l = iota((16, LANES), 0), iota((16, LANES), 1)

    def edge_start(kind, layer, b, columns):
        lane = e_r + (LANES - edge) if kind == 0 else e_r
        pick = ones_where((e_r < edge) & (e_l == lane))
        edge_out[at(kind, layer, b)] = nt(pick, columns).astype(BF)
        edge_copy(kind, layer, b).start()

    def edge_finish(kind, layer, b):
        edge_copy(kind, layer, b).wait_recv()
        lane = e_r + (LANES - edge) if kind == 0 else e_r
        there = (me_p > 0) if kind == 0 else (me_p < parts - 1)
        keep = jnp.where(there, 1.0, 0.0).astype(F32)
        pick = ones_where((e_r < edge) & (e_l == lane))
        columns = nt(c_same[...], edge_in[at(kind, layer, b)]).astype(BF)
        edge_wide[kind] = nn(columns, pick) * keep

    own_share = pl.ds(pl.multiple_of(me_p * share, share), share)
    late = layers

    def lanes_of(i):
        if i == late:
            return 0, pl.ds(2 * pair, pair)
        if i == 0:
            return 0, pl.ds(0, 2 * pair)
        return i, pl.ds(0, 3 * pair)

    def share_start(i, source, target, mine):
        layer, lanes = lanes_of(i)

        for peer, where in zip(part_peers, part_ids):
            away = pl.ds(pl.multiple_of(peer * share, share), share)
            pltpu.make_async_remote_copy(
                src_ref=source.at[layer, own_share if mine else away, lanes],
                dst_ref=target.at[layer, own_share, lanes],
                send_sem=sum_send.at[2 * i + mine],
                recv_sem=sum_recv.at[2 * i + mine],
                device_id=where,
                device_id_type=MESH,
            ).start()

    def share_copy(i, source, target, mine):
        layer, lanes = lanes_of(i)
        rest = pl.ds(0, (parts - 1) * share)
        return pltpu.make_async_remote_copy(
            src_ref=source.at[layer, rest, lanes],
            dst_ref=target.at[layer, rest, lanes],
            send_sem=sum_send.at[2 * i + mine],
            recv_sem=sum_recv.at[2 * i + mine],
            device_id=part_ids[0],
            device_id_type=MESH,
        )

    def scatter_start(i):
        layer, lanes = lanes_of(i)
        g_in[layer, own_share, lanes] = g_out[layer, own_share, lanes]
        share_start(i, g_out, g_in, 0)

    def total_up(i):
        share_copy(i, g_out, g_in, 0).wait_recv()
        layer, lanes = lanes_of(i)
        total = g_in[layer, pl.ds(0, share), lanes].astype(F32)
        for p in range(1, parts):
            total = total + g_in[layer, pl.ds(p * share, share), lanes].astype(F32)
        g_sum[layer, own_share, lanes] = (total * scale).astype(BF)
        share_start(i, g_sum, g_sum, 1)

    def taps_start():
        own = pl.ds(pl.multiple_of(me_p * 16, 16), 16)

        tp_in[own, :] = tp_out[...]
        for where in part_ids:
            pltpu.make_async_remote_copy(
                src_ref=tp_out,
                dst_ref=tp_in.at[own],
                send_sem=sum_send.at[2 * layers + 2],
                recv_sem=sum_recv.at[2 * layers + 2],
                device_id=where,
                device_id_type=MESH,
            ).start()

    def taps_copy():
        rest = pl.ds(0, (parts - 1) * 16)
        return pltpu.make_async_remote_copy(
            src_ref=tp_in.at[rest],
            dst_ref=tp_in.at[rest],
            send_sem=sum_send.at[2 * layers + 2],
            recv_sem=sum_recv.at[2 * layers + 2],
            device_id=part_ids[0],
            device_id_type=MESH,
        )

    def in_rows(step):
        def one(r, _):
            step(pl.ds(pl.multiple_of(r * ROWS, ROWS), ROWS))
            return 0

        lax.fori_loop(0, chan // ROWS, one, 0, unroll=True)

    u_f, q_f, o_f, o_b, q_b, u_b = range(6)
    last = layers - 1
    cut = width - LANES

    def stream(b, layer):
        return tok[b] if layer == 0 else xs[layer, b]

    def f1_one(b, layer, m, kind):
        sent[at(kind, layer, b)] = nn(w_pt[3 * layer + m], stream(b, layer)).astype(BF)

    def f1(b, layer):
        for m, kind in ((1, u_f), (0, q_f)):
            f1_one(b, layer, m, kind)
            regroup_start(at(kind, layer, b))

    def f2_signal(b, layer):
        i = at(u_f, layer, b)
        regroup_copy(i).wait_recv()
        tail = nn(w_qf[3 * layer + 1], got[i, :, cut:]).astype(BF)
        edge_start(0, layer, b, tail)
        us[layer, b, :, cut:] = tail
        us[layer, b, :, :cut] = nn(w_qf[3 * layer + 1], got[i, :, :cut]).astype(BF)

    def f2_query(b, layer):
        i = at(q_f, layer, b)
        regroup_copy(i).wait_recv()
        query = nn(w_qf[3 * layer], got[i]).astype(BF).astype(F32)
        opened[layer, b] = jax.nn.sigmoid(query)

    def f3(b, layer):
        edge_finish(0, layer, b)

        def step(rows):
            signal = us[layer, b, rows, :].astype(F32)
            extended = jnp.concatenate((edge_wide[0, rows, :], signal), axis=1)
            total = jnp.zeros((ROWS, width), F32)
            for i in range(ntaps):
                tap = w_taps[layer, rows, i * LANES : (i + 1) * LANES]
                tap = jnp.concatenate([tap] * (width // LANES), axis=1)
                moved = signal if i == 0 else pltpu.roll(extended, i, 1)[:, LANES:]
                total = total + tap * moved
            convolved[layer, b, rows, :] = total
            gs[layer, b, rows, :] = (opened[layer, b, rows, :] * total).astype(BF)

        in_rows(step)

    def f3_send(b, layer):
        i = at(o_f, layer, b)
        sent[i] = nn(w_pt[3 * layer + 2], gs[layer, b]).astype(BF)
        regroup_start(i)

    def f4(b, layer):
        i = at(o_f, layer, b)
        regroup_copy(i).wait_recv()
        if layer < last:
            branch = nn(w_qf[3 * layer + 2], got[i])
            xs[layer + 1, b] = (stream(b, layer).astype(F32) + branch).astype(BF)

    def b1_spread(b, layer):
        upstream = cot[b] if layer == last else flow[b].astype(BF)
        ups[at(0, layer, b)] = upstream
        sent[at(o_b, layer, b)] = nn(w_qb[3 * layer + 2], upstream).astype(BF)

    def b1(b, layer):
        b1_spread(b, layer)
        regroup_start(at(o_b, layer, b))

    def gated_back(b, layer):
        i = at(o_b, layer, b)
        regroup_copy(i).wait_recv()
        cb[b] = nn(w_p[3 * layer + 2], got[i])

    def b2_edge(b, layer):
        if layer < last:
            i = at(o_b, layer, b)
            regroup_copy(i).wait_recv()
            head = nn(w_p[3 * layer + 2], got[i, :, :LANES])
        else:
            head = cb[b, :, :LANES]
        head = head * opened[layer, b, :, :LANES]
        edge_start(1, layer, b, head.astype(BF))
        cb[b, :, :LANES] = head
        if layer < last:
            rest = nn(w_p[3 * layer + 2], got[i, :, LANES:])
        else:
            rest = cb[b, :, LANES:]
        cb[b, :, LANES:] = rest * opened[layer, b, :, LANES:]

    def b2_query(b, layer):
        def step(rows):
            shut = 1.0 - opened[layer, b, rows, :]
            back = cb[b, rows, :] * convolved[layer, b, rows, :] * shut
            ups[at(1, layer, b), rows, :] = back.astype(BF)

        in_rows(step)
        i = at(q_b, layer, b)
        sent[i] = nn(w_qb[3 * layer], ups[at(1, layer, b)]).astype(BF)
        regroup_start(i)

    def b3(b, layer):
        edge_finish(1, layer, b)

        def step(rows):
            conv_back = cb[b, rows, :]
            extended = jnp.concatenate((conv_back, edge_wide[1, rows, :]), axis=1)
            signal = us[layer, b, rows, :].astype(F32)
            total = jnp.zeros((ROWS, width), F32)
            for i in range(ntaps):
                tap = w_taps[layer, rows, i * LANES : (i + 1) * LANES]
                tap = jnp.concatenate([tap] * (width // LANES), axis=1)
                if i == 0:
                    moved = conv_back
                else:
                    moved = pltpu.roll(extended, width + LANES - i, 1)[:, :width]
                total = total + tap * moved
                term = moved * signal
                narrow = term[:, :LANES]
                for q in range(1, width // LANES):
                    narrow = narrow + term[:, q * LANES : (q + 1) * LANES]
                lanes = slice(i * LANES, (i + 1) * LANES)
                if b > 0:
                    narrow = narrow + tap_acc[rows, lanes]
                tap_acc[rows, lanes] = narrow
            ups[at(2, layer, b), rows, :] = total.astype(BF)

        in_rows(step)
        i = at(u_b, layer, b)
        sent[i] = nn(w_qb[3 * layer + 1], ups[at(2, layer, b)]).astype(BF)
        regroup_start(i)

    def b4(b, layer):
        regroup_copy(at(q_b, layer, b)).wait_recv()
        regroup_copy(at(u_b, layer, b)).wait_recv()
        back = nn(w_p[3 * layer], got[at(q_b, layer, b)])
        back = back + nn(w_p[3 * layer + 1], got[at(u_b, layer, b)])
        before = cot[b].astype(F32) if layer == last else flow[b]
        if layer > 0:
            flow[b] = before + back
        else:
            out_x[b] = (before + back).astype(BF)

    def tap_rows(layer):
        total = jnp.zeros((16, chan), F32)
        for i in range(ntaps):
            part = tap_acc[:, i * LANES : (i + 1) * LANES]
            high = part.astype(BF)
            low = (part - high.astype(F32)).astype(BF)
            row = ones_where(e_r == layer * ntaps + i)
            total = total + nt(row, high) + nt(row, low)
        if layer == last:
            tap_total[...] = total
        else:
            tap_total[...] += total

    both = range(batch)

    def first_term(half, inputs, spread):
        term = nt(inputs[0], spread[0])
        for b in range(1, batch):
            term = term + nt(inputs[b], spread[b])
        return nn(term.astype(BF) * c_mask1[...], c_pack1[half])

    def second_term(half, sections, upstream):
        term = nt(sections[0], upstream[0])
        for b in range(1, batch):
            term = term + nt(sections[b], upstream[b])
        narrow = nn(term.astype(BF) * c_mask2[...], c_pack2[half]).astype(BF)
        return nn(c_permt[...], narrow)

    def every(ref, kind, layer):
        return [ref[at(kind, layer, b)] for b in both]

    def grads_early(layer):
        second_o = second_term(1, every(got, o_f, layer), every(ups, 0, layer))
        first_o = first_term(0, [gs[layer, b] for b in both], every(got, o_b, layer))
        g_out[layer, :, :pair] = (first_o + second_o).astype(BF)
        second_q = second_term(0, every(got, q_f, layer), every(ups, 1, layer))
        second_u = second_term(1, every(got, u_f, layer), every(ups, 2, layer))
        g_out[layer, :, pair : 2 * pair] = (second_q + second_u).astype(BF)

    def grads_late(layer):
        inputs = [stream(b, layer) for b in both]
        first_q = first_term(0, inputs, every(got, q_b, layer))
        first_u = first_term(1, inputs, every(got, u_b, layer))
        g_out[layer, :, 2 * pair :] = (first_q + first_u).astype(BF)

    constants_first()
    make_pt(1)
    make_pt(0)
    for b in both:
        f1_one(b, 0, 1, u_f)
        f1_one(b, 0, 0, q_f)
    constants_second()
    pl.semaphore_wait(barrier, nh - 1 + parts - 1)
    for b in both:
        regroup_start(at(u_f, 0, b))
        regroup_start(at(q_f, 0, b))
    make_q(3 * last + 2)
    for b in both:
        b1(b, last)
    make_q(1)
    make_q(0)
    make_taps(0)
    make_pt(2)
    make_q(2)
    for layer in range(layers):
        if layer == last:
            for m in range(2):
                make_p(3 * last + m)
        for b in both:
            f2_signal(b, layer)
            if b == 0:
                f2_query(b, layer)
                if layer == last:
                    b2_edge(b, layer)
        for b in both:
            if b > 0:
                f2_query(b, layer)
                if layer == last:
                    b2_edge(b, layer)
            f3(b, layer)
            if layer < last:
                f3_send(b, layer)
            else:
                b2_query(b, layer)
                b3(b, layer)
        if layer < last:
            for m in range(3):
                make_pt(3 * layer + 3 + m)
            for b in both:
                f4(b, layer)
                f1(b, layer + 1)
            for m in range(3):
                if layer + 1 < last or m < 2:
                    make_q(3 * layer + 3 + m)
            make_taps(layer + 1)
            if layer == 0:
                constants_last()
                make_p(3 * last + 2)
                for b in both:
                    gated_back(b, last)
    for b in both:
        f3_send(b, last)
    for layer in reversed(range(layers)):
        if layer < last:
            b2_edge(0, layer)
            b2_query(0, layer)
            for b in range(1, batch):
                b2_edge(b, layer)
            for b in both:
                if b > 0:
                    b2_query(b, layer)
                b3(b, layer)
        tap_rows(layer)
        if layer == 0:
            tp_out[...] = tap_total[...].astype(BF)
            taps_start()
        if layer == last:
            for b in both:
                f4(b, last)
        grads_early(layer)
        if layer == 0:
            scatter_start(0)
        if layer > 0:
            make_p(3 * layer - 1)
            for b in both:
                b4(b, layer)
                b1(b, layer - 1)
            grads_late(layer)
            scatter_start(layer)
            for m in range(2):
                make_p(3 * layer - 3 + m)
        if 0 < layer < last:
            total_up(layer + 1)
    total_up(1)
    for b in both:
        regroup_copy(at(q_b, 0, b)).wait_recv()
        regroup_copy(at(u_b, 0, b)).wait_recv()
    grads_late(0)
    scatter_start(late)
    for b in both:
        back = nn(w_p[0], got[at(q_b, 0, b)]) + nn(w_p[1], got[at(u_b, 0, b)])
        out_x[b] = (flow[b] + back).astype(BF)
    total_up(0)
    taps_copy().wait_recv()
    total = tp_in[:16, :].astype(F32)
    for p in range(1, parts):
        total = total + tp_in[p * 16 : (p + 1) * 16, :].astype(F32)
    total = (total * scale).astype(BF)
    for layer in range(layers):
        out_taps[layer] = total[layer * ntaps : (layer + 1) * ntaps, :]
    total_up(late)

    for i in range(6 * layers * batch):
        regroup_copy(i).wait_send()
    for layer in range(layers):
        for b in both:
            edge_copy(0, layer, b).wait_send()
            edge_copy(1, layer, b).wait_send()
    taps_copy().wait_send()
    for i in range(layers + 1):
        share_copy(i, g_out, g_in, 0).wait_send()
        share_copy(i, g_sum, g_sum, 1).wait()


def unpack(nb, projections, x, sums, tap, out_x, out_first, out_second, out_taps, held, sems):
    load = pltpu.make_async_copy(sums, held, sems.at[0])
    load.start()
    whole_x = pltpu.make_async_copy(x, out_x, sems.at[1])
    whole_x.start()
    out_taps[...] = tap[...]
    load.wait()
    for layer in range(sums.shape[0]):
        for m in range(projections):
            one = (4 + m if m < 2 else 0) * nb
            two = (2 + m if m < 2 else 1) * nb
            out_first[projections * layer + m] = held[layer, :, one : one + nb]
            out_second[projections * layer + m] = held[layer, :, two : two + nb]
    whole_x.wait()


def body(sizes, tokens, cotangent, first_factors, second_factors, conv_taps):
    nh, nz, ns = sizes
    batch, chan, width = tokens.shape
    layers, ntaps, _ = conv_taps.shape
    nb = first_factors.shape[3]
    projections = first_factors.shape[1]
    parts = nz * ns
    share = chan // parts
    pair = 2 * nb
    many = layers * projections
    dims = (layers, ntaps, batch, chan, width, nb, nh, nz, ns)
    V = pltpu.VMEM
    sq = (chan, chan)
    act = (layers, batch, chan, width)
    regroups = 6 * layers * batch
    grad = (layers, chan, projections * pair)
    scratch = [
        V((chan, nb), BF),
        V((chan, nb), BF),
        V(sq, BF),
        V(sq, BF),
        V(sq, BF),
        V(sq, BF),
        V(sq, BF),
        V(sq, BF),
        V((2, chan, pair), BF),
        V((2, chan, pair), BF),
        V(sq, BF),
        V((many,) + sq, BF),
        V((many,) + sq, BF),
        V((many,) + sq, BF),
        V((many,) + sq, BF),
        V((layers, chan, ntaps * LANES), F32),
        V(act, BF),
        V(act, BF),
        V(act, BF),
        V(act, F32),
        V(act, F32),
        V((3 * layers * batch, chan, width), BF),
        V((batch, chan, width), F32),
        V((batch, chan, width), F32),
        V((regroups, chan, width), BF),
        V((regroups, chan, width), BF),
        V((2 * layers * batch, 16, chan), BF),
        V((2 * layers * batch, 16, chan), BF),
        V((2, chan, LANES), F32),
        V((chan, ntaps * LANES), F32),
        V(grad, BF),
        V((layers, parts * share, projections * pair), BF),
        V((16, chan), BF),
        V((parts * 16, chan), BF),
        V((16, chan), F32),
        pltpu.SemaphoreType.DMA((regroups,)),
        pltpu.SemaphoreType.DMA((regroups,)),
        pltpu.SemaphoreType.DMA((2 * layers * batch,)),
        pltpu.SemaphoreType.DMA((2 * layers * batch,)),
        pltpu.SemaphoreType.DMA((2 * layers + 3,)),
        pltpu.SemaphoreType.DMA((2 * layers + 3,)),
    ]
    whole = pl.BlockSpec(memory_space=pltpu.VMEM)
    anywhere = pl.BlockSpec(memory_space=pl.ANY)
    x_shape = jax.ShapeDtypeStruct((batch, chan, width), BF)
    factor_shape = jax.ShapeDtypeStruct((many, chan, nb), BF)
    taps_shape = jax.ShapeDtypeStruct((layers, ntaps, chan), BF)
    moved = pl.pallas_call(
        functools.partial(kernel, dims),
        out_shape=(x_shape, jax.ShapeDtypeStruct(grad, BF), taps_shape),
        in_specs=[whole] * 5,
        out_specs=[whole] * 3,
        scratch_shapes=scratch,
        compiler_params=pltpu.CompilerParams(
            collective_id=0, has_side_effects=True, vmem_limit_bytes=56 * 1024 * 1024
        ),
    )(
        tokens,
        cotangent,
        first_factors.reshape(many, chan, nb),
        second_factors.reshape(many, chan, nb),
        conv_taps,
    )
    out_x, out_first, out_second, out_taps = pl.pallas_call(
        functools.partial(unpack, nb, projections),
        out_shape=(x_shape, factor_shape, factor_shape, taps_shape),
        in_specs=[anywhere, anywhere, whole],
        out_specs=[whole] * 4,
        scratch_shapes=[V(grad, BF), pltpu.SemaphoreType.DMA((2,))],
        compiler_params=pltpu.CompilerParams(vmem_limit_bytes=56 * 1024 * 1024),
    )(*moved)
    return (
        out_x,
        out_first.reshape(first_factors.shape),
        out_second.reshape(second_factors.shape),
        out_taps,
    )


def solution(mesh):
    sizes = (mesh.shape["hid"], mesh.shape["dp"], mesh.shape["seq"])
    return jax.shard_map(
        functools.partial(body, sizes),
        mesh=mesh,
        in_specs=(
            P(None, "hid", ("dp", "seq")),
            P(None, "hid", ("dp", "seq")),
            P(None, None, "hid", None, None),
            P(None, None, "hid", None, None),
            P(None, None, "hid"),
        ),
        out_specs=(
            P(None, "hid", ("dp", "seq")),
            P(None, None, "hid", None, None),
            P(None, None, "hid", None, None),
            P(None, None, "hid"),
        ),
        check_vma=False,
    )
```

```python
import functools
import math

import jax
import jax.numpy as jnp
from jax import lax
from jax.experimental import pallas as pl
from jax.experimental.pallas import tpu as pltpu
from jax.sharding import PartitionSpec as P

MESH = pl.DeviceIdType.MESH
BF = jnp.bfloat16
F32 = jnp.float32
LANES = 128
ROWS = 32


def iota(shape, dim):
    return lax.broadcasted_iota(jnp.int32, shape, dim)


def nn(a, b):
    return lax.dot_general(a, b, (((1,), (0,)), ((), ())), preferred_element_type=F32)


def nt(a, b):
    return lax.dot_general(a, b, (((1,), (1,)), ((), ())), preferred_element_type=F32)


def ones_where(condition):
    return jnp.where(condition, 1.0, 0.0).astype(BF)


def kernel(
    dims,
    tok,
    cot,
    first,
    second,
    taps,
    out_x,
    g_sum,
    out_taps,
    c_exp1,
    c_exp2,
    c_mask1,
    c_mask1t,
    c_mask2,
    c_mask2t,
    c_perm,
    c_permt,
    c_pack1,
    c_pack2,
    c_same,
    w_p,
    w_pt,
    w_qf,
    w_qb,
    w_taps,
    xs,
    us,
    gs,
    opened,
    convolved,
    ups,
    flow,
    cb,
    sent,
    got,
    edge_out,
    edge_in,
    edge_wide,
    tap_acc,
    g_out,
    g_pair,
    g_half,
    g_in,
    tp_out,
    tp_in,
    tap_total,
    reg_send,
    reg_recv,
    edge_send,
    edge_recv,
    sum_send,
    sum_recv,
):
    layers, ntaps, batch, chan, width, nb, nh, nz, ns = dims
    nx = int(math.isqrt(nh))
    ny = nh // nx
    parts = nz * ns
    block = chan // nh
    share = chan // parts
    pair = 2 * nb
    scale = 1.0 / math.sqrt(batch * parts * width)

    me_h = lax.axis_index("hid")
    me_y, me_x = me_h // nx, me_h % nx
    me_z, me_c = lax.axis_index("dp"), lax.axis_index("seq")
    me_p = me_z * ns + me_c

    def far(k, n):
        return min(k, n - k)

    def hid_at(h):
        return (me_z, me_c, h)

    def part_at(p):
        return (p // ns, p % ns, me_h)

    turns = [(dy, dx) for dy in range(ny) for dx in range(nx) if dy + dx > 0]
    turns.sort(key=lambda t: -far(t[0], ny) - far(t[1], nx))
    peers_y = [(me_y + dy) % ny * nx for dy in range(ny)]
    peers_x = [(me_x + dx) % nx for dx in range(nx)]
    hid_peers = [peers_y[dy] + peers_x[dx] for dy, dx in turns]
    steps = sorted(range(1, parts), key=lambda k: -far(k, parts))
    part_peers = [(me_p + k) % parts for k in steps]
    part_ids = [part_at(p) for p in part_peers]

    barrier = pltpu.get_barrier_semaphore()

    for h in hid_peers:
        pl.semaphore_signal(barrier, inc=1, device_id=hid_at(h), device_id_type=MESH)
    for where in part_ids:
        pl.semaphore_signal(barrier, inc=1, device_id=where, device_id_type=MESH)

    nb_shift = nb.bit_length() - 1
    r_c, k_c = iota((chan, nb), 0), iota((chan, nb), 1)
    r_s, c_s = iota((chan, chan), 0), iota((chan, chan), 1)
    r_p, k_p = iota((chan, pair), 0), iota((chan, pair), 1)

    def constants_first():
        c_exp1[...] = ones_where(k_c == ((r_c >> 4) << 2) + (r_c & 3))
        c_mask1t[...] = ones_where(((r_s >> 2) & 3) == (c_s >> nb_shift))

    def constants_second():
        c_exp2[...] = ones_where(k_c == (r_c & (nb - 1)))
        c_perm[...] = ones_where(c_s == ((r_s & 3) << nb_shift) + (r_s >> 2))
        c_mask2[...] = ones_where((r_s & 3) == (c_s >> nb_shift))
        c_mask2t[...] = ones_where((c_s & 3) == (r_s >> nb_shift))
        c_same[...] = ones_where(r_s == c_s)

    def constants_last():
        c_mask1[...] = ones_where(((c_s >> 2) & 3) == (r_s >> nb_shift))
        c_permt[...] = ones_where(r_s == ((c_s & 3) << nb_shift) + (c_s >> 2))
        for half in range(2):
            to1 = half * nb + ((r_p >> 4) << 2) + (r_p & 3)
            c_pack1[half] = ones_where(k_p == to1)
            c_pack2[half] = ones_where(k_p == half * nb + (r_p & (nb - 1)))

    def make_pt(i):
        w_pt[i] = nt(c_exp1[...], first[i]).astype(BF) * c_mask1t[...]

    def make_p(i):
        w_p[i] = nt(first[i], c_exp1[...]).astype(BF) * c_mask1[...]

    def make_q(i):
        rows = nn(c_perm[...], second[i]).astype(BF)
        w_qb[i] = nt(rows, c_exp2[...]).astype(BF) * c_mask2[...]
        w_qf[i] = nt(c_exp2[...], rows).astype(BF) * c_mask2t[...]

    def make_taps(layer):
        columns = nt(c_same[...], taps[layer]).astype(BF)
        lane = iota((ntaps, ntaps * LANES), 1) >> 7
        spread = ones_where(lane == iota((ntaps, ntaps * LANES), 0))
        w_taps[layer] = nn(columns, spread)

    own_rows = pl.ds(pl.multiple_of(me_h * block, block), block)

    def at(kind, layer, b):
        return (kind * layers + layer) * batch + b

    def regroup_start(i):
        got[i, own_rows, :] = sent[i, own_rows, :]

        for peer in hid_peers:
            pltpu.make_async_remote_copy(
                src_ref=sent.at[i, pl.ds(pl.multiple_of(peer * block, block), block)],
                dst_ref=got.at[i, own_rows],
                send_sem=reg_send.at[i],
                recv_sem=reg_recv.at[i],
                device_id=hid_at(peer),
                device_id_type=MESH,
            ).start()

    def regroup_copy(i):
        rest = pl.ds(0, (nh - 1) * block)
        return pltpu.make_async_remote_copy(
            src_ref=sent.at[i, rest],
            dst_ref=got.at[i, rest],
            send_sem=reg_send.at[i],
            recv_sem=reg_recv.at[i],
            device_id=hid_at(hid_peers[0]),
            device_id_type=MESH,
        )

    edge = ntaps - 1

    def edge_copy(kind, layer, b):
        i = at(kind, layer, b)
        step = steps.index(1 if kind == 0 else parts - 1)
        return pltpu.make_async_remote_copy(
            src_ref=edge_out.at[i],
            dst_ref=edge_in.at[i],
            send_sem=edge_send.at[i],
            recv_sem=edge_recv.at[i],
            device_id=part_ids[step],
            device_id_type=MESH,
        )

    e_r, e_l = iota((16, LANES), 0), iota((16, LANES), 1)

    def edge_start(kind, layer, b, columns):
        lane = e_r + (LANES - edge) if kind == 0 else e_r
        pick = ones_where((e_r < edge) & (e_l == lane))
        edge_out[at(kind, layer, b)] = nt(pick, columns).astype(BF)
        edge_copy(kind, layer, b).start()

    def edge_finish(kind, layer, b):
        edge_copy(kind, layer, b).wait_recv()
        lane = e_r + (LANES - edge) if kind == 0 else e_r
        there = (me_p > 0) if kind == 0 else (me_p < parts - 1)
        keep = jnp.where(there, 1.0, 0.0).astype(F32)
        pick = ones_where((e_r < edge) & (e_l == lane))
        columns = nt(c_same[...], edge_in[at(kind, layer, b)]).astype(BF)
        edge_wide[kind] = nn(columns, pick) * keep

    own_share = pl.ds(pl.multiple_of(me_p * share, share), share)
    half = nz * share
    own_half = pl.ds(pl.multiple_of(me_c * half, half), half)
    other_half = pl.ds(pl.multiple_of((ns - 1 - me_c) * half, half), half)
    own_slot = pl.ds(pl.multiple_of(me_z * share, share), share)
    own_part = pl.ds(pl.multiple_of(me_c * half + me_z * share, share), share)
    rest_slots = pl.ds(0, (nz - 1) * share)
    sibling = (me_z, ns - 1 - me_c, me_h)
    steps_z = sorted(range(1, nz), key=lambda k: -far(k, nz))
    peers_z = [(me_z + k) % nz for k in steps_z]
    late = 4 * layers

    def lanes_of(layer):
        return pl.ds(0, (2 if layer == 0 else 3) * pair)

    def sum_copy(sem, source, target, where):
        return pltpu.make_async_remote_copy(
            src_ref=source,
            dst_ref=target,
            send_sem=sum_send.at[sem],
            recv_sem=sum_recv.at[sem],
            device_id=where,
            device_id_type=MESH,
        )

    def pair_copy(layer):
        lanes = lanes_of(layer)
        source = g_out.at[layer, other_half, lanes]
        return sum_copy(4 * layer, source, g_pair.at[layer, pl.ds(0, half), lanes], sibling)

    def slots_copy(layer):
        lanes = lanes_of(layer)
        source = g_half.at[layer, rest_slots, lanes]
        target = g_in.at[layer, rest_slots, lanes]
        return sum_copy(4 * layer + 1, source, target, (peers_z[0], me_c, me_h))

    def parts_copy(layer):
        rows = g_sum.at[layer, rest_slots, lanes_of(layer)]
        return sum_copy(4 * layer + 2, rows, rows, (peers_z[0], me_c, me_h))

    def back_copy(layer):
        rows = g_sum.at[layer, own_half, lanes_of(layer)]
        return sum_copy(4 * layer + 3, rows, rows, sibling)

    def pair_up(layer):
        pair_copy(layer).wait_recv()
        lanes = lanes_of(layer)
        total = g_out[layer, own_half, lanes].astype(F32)
        total = total + g_pair[layer, pl.ds(0, half), lanes].astype(F32)
        g_half[layer, pl.ds(0, half), lanes] = total.astype(BF)
        g_in[layer, own_slot, lanes] = g_half[layer, own_slot, lanes]
        for z in peers_z:
            away = pl.ds(pl.multiple_of(z * share, share), share)
            source = g_half.at[layer, away, lanes]
            target = g_in.at[layer, own_slot, lanes]
            sum_copy(4 * layer + 1, source, target, (z, me_c, me_h)).start()

    def total_up(layer):
        slots_copy(layer).wait_recv()
        lanes = lanes_of(layer)
        total = g_in[layer, pl.ds(0, share), lanes].astype(F32)
        for z in range(1, nz):
            total = total + g_in[layer, pl.ds(z * share, share), lanes].astype(F32)
        g_sum[layer, own_part, lanes] = (total * scale).astype(BF)
        rows = g_sum.at[layer, own_part, lanes]
        for z in peers_z:
            sum_copy(4 * layer + 2, rows, rows, (z, me_c, me_h)).start()

    def hand_back(layer):
        parts_copy(layer).wait_recv()
        back_copy(layer).start()

    late_lanes = pl.ds(2 * pair, pair)

    def late_copy(source, target, back):
        rest = pl.ds(0, (parts - 1) * share)
        one, two = source.at[0, rest, late_lanes], target.at[0, rest, late_lanes]
        return sum_copy(late + back, one, two, part_ids[0])

    def late_scatter():
        g_in[0, own_share, late_lanes] = g_out[0, own_share, late_lanes]
        target = g_in.at[0, own_share, late_lanes]
        for peer, where in zip(part_peers, part_ids):
            away = pl.ds(pl.multiple_of(peer * share, share), share)
            sum_copy(late, g_out.at[0, away, late_lanes], target, where).start()

    def late_total():
        late_copy(g_out, g_in, 0).wait_recv()
        total = g_in[0, pl.ds(0, share), late_lanes].astype(F32)
        for p in range(1, parts):
            total = total + g_in[0, pl.ds(p * share, share), late_lanes].astype(F32)
        g_sum[0, own_share, late_lanes] = (total * scale).astype(BF)
        rows = g_sum.at[0, own_share, late_lanes]
        for where in part_ids:
            sum_copy(late + 1, rows, rows, where).start()

    def taps_start(tile):
        own = pl.ds(pl.multiple_of(me_p * 16, 16), 16)
        tp_in[tile, own, :] = tp_out[tile]
        for where in part_ids:
            sum_copy(late + 2 + tile, tp_out.at[tile], tp_in.at[tile, own], where).start()

    def taps_copy(tile):
        rest = tp_in.at[tile, pl.ds(0, (parts - 1) * 16)]
        return sum_copy(late + 2 + tile, rest, rest, part_ids[0])

    def taps_total(tile):
        taps_copy(tile).wait_recv()
        total = tp_in[tile, pl.ds(0, 16), :].astype(F32)
        for p in range(1, parts):
            total = total + tp_in[tile, pl.ds(p * 16, 16), :].astype(F32)
        total = (total * scale).astype(BF)
        for layer in range(layers):
            if (layer == 0) == (tile == 1):
                for side in range(2):
                    row = taps_row(layer) + side * ntaps
                    lanes = slice(side * tap_width, (side + 1) * tap_width)
                    out_taps[layer, :, lanes] = total[row : row + ntaps, :]

    tap_width = chan // 2

    def taps_row(layer):
        return 0 if layer == 0 else (layers - 1 - layer) * 2 * ntaps

    def in_rows(step):
        def one(r, _):
            step(pl.ds(pl.multiple_of(r * ROWS, ROWS), ROWS))
            return 0

        lax.fori_loop(0, chan // ROWS, one, 0, unroll=True)

    u_f, q_f, o_f, o_b, q_b, u_b = range(6)
    last = layers - 1
    cut = width - LANES

    def stream(b, layer):
        return tok[b] if layer == 0 else xs[layer, b]

    def f1_one(b, layer, m, kind):
        sent[at(kind, layer, b)] = nn(w_pt[3 * layer + m], stream(b, layer)).astype(BF)

    def f1(b, layer):
        for m, kind in ((1, u_f), (0, q_f)):
            f1_one(b, layer, m, kind)
            regroup_start(at(kind, layer, b))

    def f2_signal(b, layer):
        i = at(u_f, layer, b)
        regroup_copy(i).wait_recv()
        tail = nn(w_qf[3 * layer + 1], got[i, :, cut:]).astype(BF)
        edge_start(0, layer, b, tail)
        us[layer, b, :, cut:] = tail
        us[layer, b, :, :cut] = nn(w_qf[3 * layer + 1], got[i, :, :cut]).astype(BF)

    def f2_query(b, layer):
        i = at(q_f, layer, b)
        regroup_copy(i).wait_recv()
        query = nn(w_qf[3 * layer], got[i]).astype(BF).astype(F32)
        opened[layer, b] = jax.nn.sigmoid(query)

    def f3(b, layer):
        edge_finish(0, layer, b)

        def step(rows):
            signal = us[layer, b, rows, :].astype(F32)
            extended = jnp.concatenate((edge_wide[0, rows, :], signal), axis=1)
            total = jnp.zeros((ROWS, width), F32)
            for i in range(ntaps):
                tap = w_taps[layer, rows, i * LANES : (i + 1) * LANES]
                tap = jnp.concatenate([tap] * (width // LANES), axis=1)
                moved = signal if i == 0 else pltpu.roll(extended, i, 1)[:, LANES:]
                total = total + tap * moved
            convolved[layer, b, rows, :] = total
            gs[layer, b, rows, :] = (opened[layer, b, rows, :] * total).astype(BF)

        in_rows(step)

    def f3_send(b, layer):
        i = at(o_f, layer, b)
        sent[i] = nn(w_pt[3 * layer + 2], gs[layer, b]).astype(BF)
        regroup_start(i)

    def f4(b, layer):
        i = at(o_f, layer, b)
        regroup_copy(i).wait_recv()
        if layer < last:
            branch = nn(w_qf[3 * layer + 2], got[i])
            xs[layer + 1, b] = (stream(b, layer).astype(F32) + branch).astype(BF)

    def b1_spread(b, layer):
        upstream = cot[b] if layer == last else flow[b].astype(BF)
        ups[at(0, layer, b)] = upstream
        sent[at(o_b, layer, b)] = nn(w_qb[3 * layer + 2], upstream).astype(BF)

    def b1(b, layer):
        b1_spread(b, layer)
        regroup_start(at(o_b, layer, b))

    def gated_back(b, layer):
        i = at(o_b, layer, b)
        regroup_copy(i).wait_recv()
        cb[b] = nn(w_p[3 * layer + 2], got[i])

    def b2_edge(b, layer):
        if layer < last:
            i = at(o_b, layer, b)
            regroup_copy(i).wait_recv()
            head = nn(w_p[3 * layer + 2], got[i, :, :LANES])
        else:
            head = cb[b, :, :LANES]
        head = head * opened[layer, b, :, :LANES]
        edge_start(1, layer, b, head.astype(BF))
        cb[b, :, :LANES] = head
        if layer < last:
            rest = nn(w_p[3 * layer + 2], got[i, :, LANES:])
        else:
            rest = cb[b, :, LANES:]
        cb[b, :, LANES:] = rest * opened[layer, b, :, LANES:]

    def b2_query(b, layer):
        def step(rows):
            shut = 1.0 - opened[layer, b, rows, :]
            back = cb[b, rows, :] * convolved[layer, b, rows, :] * shut
            ups[at(1, layer, b), rows, :] = back.astype(BF)

        in_rows(step)
        i = at(q_b, layer, b)
        sent[i] = nn(w_qb[3 * layer], ups[at(1, layer, b)]).astype(BF)
        regroup_start(i)

    def b3(b, layer):
        edge_finish(1, layer, b)

        def step(rows):
            conv_back = cb[b, rows, :]
            extended = jnp.concatenate((conv_back, edge_wide[1, rows, :]), axis=1)
            signal = us[layer, b, rows, :].astype(F32)
            total = jnp.zeros((ROWS, width), F32)
            for i in range(ntaps):
                tap = w_taps[layer, rows, i * LANES : (i + 1) * LANES]
                tap = jnp.concatenate([tap] * (width // LANES), axis=1)
                if i == 0:
                    moved = conv_back
                else:
                    moved = pltpu.roll(extended, width + LANES - i, 1)[:, :width]
                total = total + tap * moved
                term = moved * signal
                narrow = term[:, :LANES]
                for q in range(1, width // LANES):
                    narrow = narrow + term[:, q * LANES : (q + 1) * LANES]
                lanes = slice(i * LANES, (i + 1) * LANES)
                if b > 0:
                    narrow = narrow + tap_acc[rows, lanes]
                tap_acc[rows, lanes] = narrow
            ups[at(2, layer, b), rows, :] = total.astype(BF)

        in_rows(step)
        i = at(u_b, layer, b)
        sent[i] = nn(w_qb[3 * layer + 1], ups[at(2, layer, b)]).astype(BF)
        regroup_start(i)

    def b4(b, layer):
        regroup_copy(at(q_b, layer, b)).wait_recv()
        regroup_copy(at(u_b, layer, b)).wait_recv()
        back = nn(w_p[3 * layer], got[at(q_b, layer, b)])
        back = back + nn(w_p[3 * layer + 1], got[at(u_b, layer, b)])
        before = cot[b].astype(F32) if layer == last else flow[b]
        if layer > 0:
            flow[b] = before + back
        else:
            out_x[b] = (before + back).astype(BF)

    def tap_rows(layer):
        total = jnp.zeros((16, tap_width), F32)
        for i in range(ntaps):
            for side in range(2):
                rows = slice(side * tap_width, (side + 1) * tap_width)
                part = tap_acc[rows, i * LANES : (i + 1) * LANES]
                high = part.astype(BF)
                low = (part - high.astype(F32)).astype(BF)
                row = ones_where(e_r == taps_row(layer) + side * ntaps + i)
                total = total + nt(row, high) + nt(row, low)
        if layer == last:
            tap_total[...] = total
        elif layer > 0:
            tap_total[...] += total
        if layer == 1:
            tp_out[0] = tap_total[...].astype(BF)
            taps_start(0)
        if layer == 0:
            tp_out[1] = total.astype(BF)
            taps_start(1)

    both = range(batch)

    def first_term(half, inputs, spread):
        term = nt(inputs[0], spread[0])
        for b in range(1, batch):
            term = term + nt(inputs[b], spread[b])
        return nn(term.astype(BF) * c_mask1[...], c_pack1[half])

    def second_term(half, sections, upstream):
        term = nt(sections[0], upstream[0])
        for b in range(1, batch):
            term = term + nt(sections[b], upstream[b])
        narrow = nn(term.astype(BF) * c_mask2[...], c_pack2[half]).astype(BF)
        return nn(c_permt[...], narrow)

    def every(ref, kind, layer):
        return [ref[at(kind, layer, b)] for b in both]

    def grads_o(layer):
        second_o = second_term(1, every(got, o_f, layer), every(ups, 0, layer))
        first_o = first_term(0, [gs[layer, b] for b in both], every(got, o_b, layer))
        g_out[layer, :, :pair] = (first_o + second_o).astype(BF)

    def grads_second(layer):
        second_q = second_term(0, every(got, q_f, layer), every(ups, 1, layer))
        second_u = second_term(1, every(got, u_f, layer), every(ups, 2, layer))
        g_out[layer, :, pair : 2 * pair] = (second_q + second_u).astype(BF)

    def grads_late(layer):
        inputs = [stream(b, layer) for b in both]
        first_q = first_term(0, inputs, every(got, q_b, layer))
        first_u = first_term(1, inputs, every(got, u_b, layer))
        g_out[layer, :, 2 * pair :] = (first_q + first_u).astype(BF)

    constants_first()
    make_pt(1)
    make_pt(0)
    for b in both:
        f1_one(b, 0, 1, u_f)
        f1_one(b, 0, 0, q_f)
    constants_second()
    pl.semaphore_wait(barrier, nh - 1 + parts - 1)
    for b in both:
        regroup_start(at(u_f, 0, b))
        regroup_start(at(q_f, 0, b))
    make_q(3 * last + 2)
    for b in both:
        b1(b, last)
    make_q(1)
    make_q(0)
    make_taps(0)
    make_pt(2)
    make_q(2)
    for layer in range(layers):
        if layer == last:
            for m in range(2):
                make_p(3 * last + m)
        for b in both:
            f2_signal(b, layer)
            if b == 0:
                f2_query(b, layer)
                if layer == last:
                    b2_edge(b, layer)
        for b in both:
            if b > 0:
                f2_query(b, layer)
                if layer == last:
                    b2_edge(b, layer)
            f3(b, layer)
            if layer < last:
                f3_send(b, layer)
            else:
                b2_query(b, layer)
                b3(b, layer)
        if layer < last:
            for m in range(3):
                make_pt(3 * layer + 3 + m)
            for b in both:
                f4(b, layer)
                f1(b, layer + 1)
            for m in range(3):
                if layer + 1 < last or m < 2:
                    make_q(3 * layer + 3 + m)
            make_taps(layer + 1)
            if layer == 0:
                constants_last()
                make_p(3 * last + 2)
                for b in both:
                    gated_back(b, last)
    for b in both:
        f3_send(b, last)
    for layer in reversed(range(layers)):
        if layer < last:
            b2_edge(0, layer)
            b2_query(0, layer)
            for b in range(1, batch):
                b2_edge(b, layer)
            for b in both:
                if b > 0:
                    b2_query(b, layer)
                b3(b, layer)
        tap_rows(layer)
        if layer > 0:
            make_p(3 * layer - 1)
            grads_second(layer)
            if layer < last:
                pair_up(layer + 1)
            for b in both:
                b4(b, layer)
                b1(b, layer - 1)
            if layer == last:
                for b in both:
                    f4(b, last)
            grads_o(layer)
            grads_late(layer)
            pair_copy(layer).start()
            for m in range(2):
                make_p(3 * layer - 3 + m)
            if layer < last:
                total_up(layer + 1)
        else:
            grads_o(0)
            grads_second(0)
            pair_copy(0).start()
            pair_up(1)
            hand_back(2)
            pair_up(0)
    for b in both:
        regroup_copy(at(q_b, 0, b)).wait_recv()
        regroup_copy(at(u_b, 0, b)).wait_recv()
    grads_late(0)
    late_scatter()
    for b in both:
        back = nn(w_p[0], got[at(q_b, 0, b)]) + nn(w_p[1], got[at(u_b, 0, b)])
        out_x[b] = (flow[b] + back).astype(BF)
    total_up(1)
    total_up(0)
    taps_total(0)
    taps_total(1)

    for i in range(6 * layers * batch):
        regroup_copy(i).wait_send()
    for layer in range(layers):
        for b in both:
            edge_copy(0, layer, b).wait_send()
            edge_copy(1, layer, b).wait_send()
        pair_copy(layer).wait_send()
        slots_copy(layer).wait_send()
    taps_copy(0).wait_send()
    taps_copy(1).wait_send()
    late_total()
    hand_back(1)
    hand_back(0)
    late_copy(g_out, g_in, 0).wait_send()
    for layer in range(layers):
        parts_copy(layer).wait_send()
        back_copy(layer).wait()
    late_copy(g_sum, g_sum, 1).wait()


def unpack(nb, projections, x, sums, tap, out_x, out_first, out_second, out_taps, held, sems):
    load = pltpu.make_async_copy(sums, held, sems.at[0])
    load.start()
    whole_x = pltpu.make_async_copy(x, out_x, sems.at[1])
    whole_x.start()
    out_taps[...] = tap[...]
    load.wait()
    for layer in range(sums.shape[0]):
        for m in range(projections):
            one = (4 + m if m < 2 else 0) * nb
            two = (2 + m if m < 2 else 1) * nb
            out_first[projections * layer + m] = held[layer, :, one : one + nb]
            out_second[projections * layer + m] = held[layer, :, two : two + nb]
    whole_x.wait()


def body(sizes, tokens, cotangent, first_factors, second_factors, conv_taps):
    nh, nz, ns = sizes
    batch, chan, width = tokens.shape
    layers, ntaps, _ = conv_taps.shape
    nb = first_factors.shape[3]
    projections = first_factors.shape[1]
    parts = nz * ns
    share = chan // parts
    pair = 2 * nb
    many = layers * projections
    dims = (layers, ntaps, batch, chan, width, nb, nh, nz, ns)
    V = pltpu.VMEM
    sq = (chan, chan)
    act = (layers, batch, chan, width)
    regroups = 6 * layers * batch
    grad = (layers, chan, projections * pair)
    scratch = [
        V((chan, nb), BF),
        V((chan, nb), BF),
        V(sq, BF),
        V(sq, BF),
        V(sq, BF),
        V(sq, BF),
        V(sq, BF),
        V(sq, BF),
        V((2, chan, pair), BF),
        V((2, chan, pair), BF),
        V(sq, BF),
        V((many,) + sq, BF),
        V((many,) + sq, BF),
        V((many,) + sq, BF),
        V((many,) + sq, BF),
        V((layers, chan, ntaps * LANES), F32),
        V(act, BF),
        V(act, BF),
        V(act, BF),
        V(act, F32),
        V(act, F32),
        V((3 * layers * batch, chan, width), BF),
        V((batch, chan, width), F32),
        V((batch, chan, width), F32),
        V((regroups, chan, width), BF),
        V((regroups, chan, width), BF),
        V((2 * layers * batch, 16, chan), BF),
        V((2 * layers * batch, 16, chan), BF),
        V((2, chan, LANES), F32),
        V((chan, ntaps * LANES), F32),
        V(grad, BF),
        V((layers, nz * share, projections * pair), BF),
        V((layers, nz * share, projections * pair), BF),
        V((layers, parts * share, projections * pair), BF),
        V((2, 16, chan // 2), BF),
        V((2, parts * 16, chan // 2), BF),
        V((16, chan // 2), F32),
        pltpu.SemaphoreType.DMA((regroups,)),
        pltpu.SemaphoreType.DMA((regroups,)),
        pltpu.SemaphoreType.DMA((2 * layers * batch,)),
        pltpu.SemaphoreType.DMA((2 * layers * batch,)),
        pltpu.SemaphoreType.DMA((4 * layers + 4,)),
        pltpu.SemaphoreType.DMA((4 * layers + 4,)),
    ]
    whole = pl.BlockSpec(memory_space=pltpu.VMEM)
    anywhere = pl.BlockSpec(memory_space=pl.ANY)
    x_shape = jax.ShapeDtypeStruct((batch, chan, width), BF)
    factor_shape = jax.ShapeDtypeStruct((many, chan, nb), BF)
    taps_shape = jax.ShapeDtypeStruct((layers, ntaps, chan), BF)
    moved = pl.pallas_call(
        functools.partial(kernel, dims),
        out_shape=(x_shape, jax.ShapeDtypeStruct(grad, BF), taps_shape),
        in_specs=[whole] * 5,
        out_specs=[whole] * 3,
        scratch_shapes=scratch,
        compiler_params=pltpu.CompilerParams(
            collective_id=0, has_side_effects=True, vmem_limit_bytes=56 * 1024 * 1024
        ),
    )(
        tokens,
        cotangent,
        first_factors.reshape(many, chan, nb),
        second_factors.reshape(many, chan, nb),
        conv_taps,
    )
    out_x, out_first, out_second, out_taps = pl.pallas_call(
        functools.partial(unpack, nb, projections),
        out_shape=(x_shape, factor_shape, factor_shape, taps_shape),
        in_specs=[anywhere, anywhere, whole],
        out_specs=[whole] * 4,
        scratch_shapes=[V(grad, BF), pltpu.SemaphoreType.DMA((2,))],
        compiler_params=pltpu.CompilerParams(vmem_limit_bytes=56 * 1024 * 1024),
    )(*moved)
    return (
        out_x,
        out_first.reshape(first_factors.shape),
        out_second.reshape(second_factors.shape),
        out_taps,
    )


def solution(mesh):
    sizes = (mesh.shape["hid"], mesh.shape["dp"], mesh.shape["seq"])
    return jax.shard_map(
        functools.partial(body, sizes),
        mesh=mesh,
        in_specs=(
            P(None, "hid", ("dp", "seq")),
            P(None, "hid", ("dp", "seq")),
            P(None, None, "hid", None, None),
            P(None, None, "hid", None, None),
            P(None, None, "hid"),
        ),
        out_specs=(
            P(None, "hid", ("dp", "seq")),
            P(None, None, "hid", None, None),
            P(None, None, "hid", None, None),
            P(None, None, "hid"),
        ),
        check_vma=False,
    )
```

```python
import functools
import math

import jax
import jax.numpy as jnp
from jax import lax
from jax.experimental import pallas as pl
from jax.experimental.pallas import tpu as pltpu
from jax.sharding import PartitionSpec as P

MESH = pl.DeviceIdType.MESH
BF = jnp.bfloat16
F32 = jnp.float32
LANES = 128
ROWS = 32


def iota(shape, dim):
    return lax.broadcasted_iota(jnp.int32, shape, dim)


def nn(a, b):
    return lax.dot_general(a, b, (((1,), (0,)), ((), ())), preferred_element_type=F32)


def nt(a, b):
    return lax.dot_general(a, b, (((1,), (1,)), ((), ())), preferred_element_type=F32)


def ones_where(condition):
    return jnp.where(condition, 1.0, 0.0).astype(BF)


def kernel(
    dims,
    tok_in,
    cot_in,
    first_in,
    second_in,
    taps,
    out_x,
    g_sum,
    out_taps,
    c_exp1,
    c_exp2,
    c_mask1,
    c_mask1t,
    c_mask2,
    c_mask2t,
    c_perm,
    c_permt,
    c_pack1,
    c_pack2,
    c_same,
    w_p,
    w_pt,
    w_qf,
    w_qb,
    w_taps,
    xs,
    us,
    gs,
    opened,
    convolved,
    ups,
    flow,
    cb,
    sent,
    got,
    edge_out,
    edge_in,
    edge_wide,
    back_tail,
    tap_acc,
    g_out,
    g_pair,
    g_half,
    g_in,
    tp_out,
    tp_in,
    tap_total,
    reg_send,
    reg_recv,
    edge_send,
    edge_recv,
    sum_send,
    sum_recv,
    tok,
    cot,
    first,
    second,
    in_sems,
):
    layers, ntaps, batch, chan, width, nb, nh, nz, ns = dims
    nx = int(math.isqrt(nh))
    ny = nh // nx
    parts = nz * ns
    block = chan // nh
    share = chan // parts
    pair = 2 * nb
    scale = 1.0 / math.sqrt(batch * parts * width)

    me_h = lax.axis_index("hid")
    me_y, me_x = me_h // nx, me_h % nx
    me_z, me_c = lax.axis_index("dp"), lax.axis_index("seq")
    me_p = me_z * ns + me_c

    def far(k, n):
        return min(k, n - k)

    def hid_at(h):
        return (me_z, me_c, h)

    def part_at(p):
        return (p // ns, p % ns, me_h)

    turns = [(dy, dx) for dy in range(ny) for dx in range(nx) if dy + dx > 0]
    turns.sort(key=lambda t: -far(t[0], ny) - far(t[1], nx))
    peers_y = [(me_y + dy) % ny * nx for dy in range(ny)]
    peers_x = [(me_x + dx) % nx for dx in range(nx)]
    hid_peers = [peers_y[dy] + peers_x[dx] for dy, dx in turns]
    steps = sorted(range(1, parts), key=lambda k: -far(k, parts))
    part_peers = [(me_p + k) % parts for k in steps]
    part_ids = [part_at(p) for p in part_peers]

    pairs = ((first_in, first), (tok_in, tok), (second_in, second), (cot_in, cot))
    loads = [pltpu.make_async_copy(a, b, in_sems.at[i]) for i, (a, b) in enumerate(pairs)]
    for load in loads:
        load.start()

    barrier = pltpu.get_barrier_semaphore()

    for h in hid_peers:
        pl.semaphore_signal(barrier, inc=1, device_id=hid_at(h), device_id_type=MESH)
    for where in part_ids:
        pl.semaphore_signal(barrier, inc=1, device_id=where, device_id_type=MESH)

    nb_shift = nb.bit_length() - 1
    r_c, k_c = iota((chan, nb), 0), iota((chan, nb), 1)
    r_s, c_s = iota((chan, chan), 0), iota((chan, chan), 1)
    r_p, k_p = iota((chan, pair), 0), iota((chan, pair), 1)

    def constants_first():
        c_exp1[...] = ones_where(k_c == ((r_c >> 4) << 2) + (r_c & 3))
        c_mask1t[...] = ones_where(((r_s >> 2) & 3) == (c_s >> nb_shift))

    def constants_second():
        c_exp2[...] = ones_where(k_c == (r_c & (nb - 1)))
        c_perm[...] = ones_where(c_s == ((r_s & 3) << nb_shift) + (r_s >> 2))
        c_mask2[...] = ones_where((r_s & 3) == (c_s >> nb_shift))
        c_mask2t[...] = ones_where((c_s & 3) == (r_s >> nb_shift))
        c_same[...] = ones_where(r_s == c_s)

    def constants_last():
        c_mask1[...] = ones_where(((c_s >> 2) & 3) == (r_s >> nb_shift))
        c_permt[...] = ones_where(r_s == ((c_s & 3) << nb_shift) + (c_s >> 2))
        for half in range(2):
            to1 = half * nb + ((r_p >> 4) << 2) + (r_p & 3)
            c_pack1[half] = ones_where(k_p == to1)
            c_pack2[half] = ones_where(k_p == half * nb + (r_p & (nb - 1)))

    def make_pt(i):
        w_pt[i] = nt(c_exp1[...], first[i]).astype(BF) * c_mask1t[...]

    def make_p(i):
        w_p[i] = nt(first[i], c_exp1[...]).astype(BF) * c_mask1[...]

    def make_q(i):
        rows = nn(c_perm[...], second[i]).astype(BF)
        w_qb[i] = nt(rows, c_exp2[...]).astype(BF) * c_mask2[...]
        w_qf[i] = nt(c_exp2[...], rows).astype(BF) * c_mask2t[...]

    def make_taps(layer):
        columns = nt(c_same[...], taps[layer]).astype(BF)
        lane = iota((ntaps, ntaps * LANES), 1) >> 7
        spread = ones_where(lane == iota((ntaps, ntaps * LANES), 0))
        w_taps[layer] = nn(columns, spread)

    own_rows = pl.ds(pl.multiple_of(me_h * block, block), block)

    def at(kind, layer, b):
        return (kind * layers + layer) * batch + b

    def regroup_start(i):
        got[i, own_rows, :] = sent[i, own_rows, :]

        for peer in hid_peers:
            pltpu.make_async_remote_copy(
                src_ref=sent.at[i, pl.ds(pl.multiple_of(peer * block, block), block)],
                dst_ref=got.at[i, own_rows],
                send_sem=reg_send.at[i],
                recv_sem=reg_recv.at[i],
                device_id=hid_at(peer),
                device_id_type=MESH,
            ).start()

    def regroup_copy(i):
        rest = pl.ds(0, (nh - 1) * block)
        return pltpu.make_async_remote_copy(
            src_ref=sent.at[i, rest],
            dst_ref=got.at[i, rest],
            send_sem=reg_send.at[i],
            recv_sem=reg_recv.at[i],
            device_id=hid_at(hid_peers[0]),
            device_id_type=MESH,
        )

    edge = ntaps - 1

    def edge_copy(kind, layer, b):
        i = at(kind, layer, b)
        step = steps.index(1 if kind == 0 else parts - 1)
        return pltpu.make_async_remote_copy(
            src_ref=edge_out.at[i],
            dst_ref=edge_in.at[i],
            send_sem=edge_send.at[i],
            recv_sem=edge_recv.at[i],
            device_id=part_ids[step],
            device_id_type=MESH,
        )

    e_r, e_l = iota((16, LANES), 0), iota((16, LANES), 1)

    def edge_start(kind, layer, b, columns, weight=None):
        lane = e_r + (LANES - edge) if kind == 0 else e_r
        pick = ones_where((e_r < edge) & (e_l == lane))
        rows = nt(pick, columns).astype(BF)
        if weight is not None:
            rows = nt(rows, weight).astype(BF)
        edge_out[at(kind, layer, b)] = rows
        edge_copy(kind, layer, b).start()

    def edge_finish(kind, layer, b):
        edge_copy(kind, layer, b).wait_recv()
        lane = e_r + (LANES - edge) if kind == 0 else e_r
        there = (me_p > 0) if kind == 0 else (me_p < parts - 1)
        keep = jnp.where(there, 1.0, 0.0).astype(F32)
        pick = ones_where((e_r < edge) & (e_l == lane))
        rows = edge_in[at(kind, layer, b)]
        wide = lax.dot_general(rows, pick, (((0,), (0,)), ((), ())), preferred_element_type=F32)
        edge_wide[kind] = wide * keep

    own_share = pl.ds(pl.multiple_of(me_p * share, share), share)
    half = nz * share
    own_half = pl.ds(pl.multiple_of(me_c * half, half), half)
    other_half = pl.ds(pl.multiple_of((ns - 1 - me_c) * half, half), half)
    own_slot = pl.ds(pl.multiple_of(me_z * share, share), share)
    own_part = pl.ds(pl.multiple_of(me_c * half + me_z * share, share), share)
    rest_slots = pl.ds(0, (nz - 1) * share)
    sibling = (me_z, ns - 1 - me_c, me_h)
    steps_z = sorted(range(1, nz), key=lambda k: -far(k, nz))
    peers_z = [(me_z + k) % nz for k in steps_z]
    late = 4 * layers

    def lanes_of(layer):
        return pl.ds(0, (2 if layer == 0 else 3) * pair)

    def sum_copy(sem, source, target, where):
        return pltpu.make_async_remote_copy(
            src_ref=source,
            dst_ref=target,
            send_sem=sum_send.at[sem],
            recv_sem=sum_recv.at[sem],
            device_id=where,
            device_id_type=MESH,
        )

    def pair_copy(layer):
        lanes = lanes_of(layer)
        source = g_out.at[layer, other_half, lanes]
        return sum_copy(4 * layer, source, g_pair.at[layer, pl.ds(0, half), lanes], sibling)

    def slots_copy(layer):
        lanes = lanes_of(layer)
        source = g_half.at[layer, rest_slots, lanes]
        target = g_in.at[layer, rest_slots, lanes]
        return sum_copy(4 * layer + 1, source, target, (peers_z[0], me_c, me_h))

    def parts_copy(layer):
        rows = g_sum.at[layer, rest_slots, lanes_of(layer)]
        return sum_copy(4 * layer + 2, rows, rows, (peers_z[0], me_c, me_h))

    def back_copy(layer):
        rows = g_sum.at[layer, own_half, lanes_of(layer)]
        return sum_copy(4 * layer + 3, rows, rows, sibling)

    def pair_up(layer):
        pair_copy(layer).wait_recv()
        lanes = lanes_of(layer)
        total = g_out[layer, own_half, lanes].astype(F32)
        total = total + g_pair[layer, pl.ds(0, half), lanes].astype(F32)
        g_half[layer, pl.ds(0, half), lanes] = total.astype(BF)
        g_in[layer, own_slot, lanes] = g_half[layer, own_slot, lanes]
        for z in peers_z:
            away = pl.ds(pl.multiple_of(z * share, share), share)
            source = g_half.at[layer, away, lanes]
            target = g_in.at[layer, own_slot, lanes]
            sum_copy(4 * layer + 1, source, target, (z, me_c, me_h)).start()

    def total_up(layer):
        slots_copy(layer).wait_recv()
        lanes = lanes_of(layer)
        total = g_in[layer, pl.ds(0, share), lanes].astype(F32)
        for z in range(1, nz):
            total = total + g_in[layer, pl.ds(z * share, share), lanes].astype(F32)
        g_sum[layer, own_part, lanes] = (total * scale).astype(BF)
        rows = g_sum.at[layer, own_part, lanes]
        for z in peers_z:
            sum_copy(4 * layer + 2, rows, rows, (z, me_c, me_h)).start()

    def hand_back(layer):
        parts_copy(layer).wait_recv()
        back_copy(layer).start()

    late_lanes = pl.ds(2 * pair, pair)

    def late_copy(source, target, back):
        rest = pl.ds(0, (parts - 1) * share)
        one, two = source.at[0, rest, late_lanes], target.at[0, rest, late_lanes]
        return sum_copy(late + back, one, two, part_ids[0])

    def late_scatter():
        g_in[0, own_share, late_lanes] = g_out[0, own_share, late_lanes]
        target = g_in.at[0, own_share, late_lanes]
        for peer, where in zip(part_peers, part_ids):
            away = pl.ds(pl.multiple_of(peer * share, share), share)
            sum_copy(late, g_out.at[0, away, late_lanes], target, where).start()

    def late_total():
        late_copy(g_out, g_in, 0).wait_recv()
        total = g_in[0, pl.ds(0, share), late_lanes].astype(F32)
        for p in range(1, parts):
            total = total + g_in[0, pl.ds(p * share, share), late_lanes].astype(F32)
        g_sum[0, own_share, late_lanes] = (total * scale).astype(BF)
        rows = g_sum.at[0, own_share, late_lanes]
        for where in part_ids:
            sum_copy(late + 1, rows, rows, where).start()

    def taps_start(tile):
        own = pl.ds(pl.multiple_of(me_p * 16, 16), 16)
        tp_in[tile, own, :] = tp_out[tile]
        for where in part_ids:
            sum_copy(late + 2 + tile, tp_out.at[tile], tp_in.at[tile, own], where).start()

    def taps_copy(tile):
        rest = tp_in.at[tile, pl.ds(0, (parts - 1) * 16)]
        return sum_copy(late + 2 + tile, rest, rest, part_ids[0])

    def taps_total(tile):
        taps_copy(tile).wait_recv()
        total = tp_in[tile, pl.ds(0, 16), :].astype(F32)
        for p in range(1, parts):
            total = total + tp_in[tile, pl.ds(p * 16, 16), :].astype(F32)
        total = (total * scale).astype(BF)
        for layer in range(layers):
            if (layer == 0) == (tile == 1):
                for side in range(2):
                    row = taps_row(layer) + side * ntaps
                    lanes = slice(side * tap_width, (side + 1) * tap_width)
                    out_taps[layer, :, lanes] = total[row : row + ntaps, :]

    tap_width = chan // 2

    def taps_row(layer):
        return 0 if layer == 0 else (layers - 1 - layer) * 2 * ntaps

    def in_rows(step):
        def one(r, _):
            step(pl.ds(pl.multiple_of(r * ROWS, ROWS), ROWS))
            return 0

        lax.fori_loop(0, chan // ROWS, one, 0, unroll=True)

    u_f, q_f, o_f, o_b, q_b, u_b = range(6)
    last = layers - 1
    cut = width - LANES

    def stream(b, layer):
        return tok[b] if layer == 0 else xs[layer, b]

    def f1_one(b, layer, m, kind):
        sent[at(kind, layer, b)] = nn(w_pt[3 * layer + m], stream(b, layer)).astype(BF)

    def f1(b, layer):
        for m, kind in ((1, u_f), (0, q_f)):
            f1_one(b, layer, m, kind)
            regroup_start(at(kind, layer, b))

    def f2_signal(b, layer):
        i = at(u_f, layer, b)
        regroup_copy(i).wait_recv()
        edge_start(0, layer, b, got[i, :, cut:], w_qf[3 * layer + 1])
        us[layer, b] = nn(w_qf[3 * layer + 1], got[i]).astype(BF)

    def f2_query(b, layer):
        i = at(q_f, layer, b)
        regroup_copy(i).wait_recv()
        query = nn(w_qf[3 * layer], got[i]).astype(BF).astype(F32)
        opened[layer, b] = jax.nn.sigmoid(query)

    def tap_of(layer, rows, i):
        return w_taps[layer, rows, i * LANES : (i + 1) * LANES]

    lane_of = iota((ROWS, LANES), 1)

    def f3_main(b, layer):
        def step(rows):
            signal = us[layer, b, rows, :].astype(F32)
            extended = jnp.concatenate((jnp.zeros((ROWS, LANES), F32), signal), axis=1)
            total = jnp.zeros((ROWS, width), F32)
            for i in range(ntaps):
                tap = jnp.concatenate([tap_of(layer, rows, i)] * (width // LANES), axis=1)
                moved = signal if i == 0 else pltpu.roll(extended, i, 1)[:, LANES:]
                total = total + tap * moved
            convolved[layer, b, rows, :] = total
            gated = opened[layer, b, rows, LANES:] * total[:, LANES:]
            gs[layer, b, rows, LANES:] = gated.astype(BF)

        in_rows(step)
        if layer < last:
            i = at(o_f, layer, b)
            sent[i, :, LANES:] = nn(w_pt[3 * layer + 2], gs[layer, b, :, LANES:]).astype(BF)

    def f3_edge(b, layer):
        edge_finish(0, layer, b)

        def step(rows):
            before = edge_wide[0, rows, :]
            more = jnp.zeros((ROWS, LANES), F32)
            for i in range(1, ntaps):
                more = more + tap_of(layer, rows, i) * pltpu.roll(before, i, 1)
            total = convolved[layer, b, rows, :LANES] + jnp.where(lane_of < edge, more, 0.0)
            convolved[layer, b, rows, :LANES] = total
            gs[layer, b, rows, :LANES] = (opened[layer, b, rows, :LANES] * total).astype(BF)

        in_rows(step)

    def f3_send(b, layer):
        i = at(o_f, layer, b)
        if layer < last:
            sent[i, :, :LANES] = nn(w_pt[3 * layer + 2], gs[layer, b, :, :LANES]).astype(BF)
        else:
            sent[i] = nn(w_pt[3 * layer + 2], gs[layer, b]).astype(BF)
        regroup_start(i)

    def f4(b, layer):
        i = at(o_f, layer, b)
        regroup_copy(i).wait_recv()
        if layer < last:
            branch = nn(w_qf[3 * layer + 2], got[i])
            xs[layer + 1, b] = (stream(b, layer).astype(F32) + branch).astype(BF)

    def b1_spread(b, layer):
        upstream = cot[b] if layer == last else flow[b].astype(BF)
        ups[at(0, layer, b)] = upstream
        sent[at(o_b, layer, b)] = nn(w_qb[3 * layer + 2], upstream).astype(BF)

    def b1(b, layer):
        b1_spread(b, layer)
        regroup_start(at(o_b, layer, b))

    def gated_back(b, layer):
        i = at(o_b, layer, b)
        regroup_copy(i).wait_recv()
        cb[b] = nn(w_p[3 * layer + 2], got[i])

    def b2_edge(b, layer):
        if layer < last:
            i = at(o_b, layer, b)
            regroup_copy(i).wait_recv()
            head = nn(w_p[3 * layer + 2], got[i, :, :LANES])
        else:
            head = cb[b, :, :LANES]
        head = head * opened[layer, b, :, :LANES]
        edge_start(1, layer, b, head.astype(BF))
        cb[b, :, :LANES] = head
        if layer < last:
            rest = nn(w_p[3 * layer + 2], got[i, :, LANES:])
        else:
            rest = cb[b, :, LANES:]
        cb[b, :, LANES:] = rest * opened[layer, b, :, LANES:]

    def b2_query(b, layer):
        def step(rows):
            shut = 1.0 - opened[layer, b, rows, :]
            back = cb[b, rows, :] * convolved[layer, b, rows, :] * shut
            ups[at(1, layer, b), rows, :] = back.astype(BF)

        in_rows(step)
        i = at(q_b, layer, b)
        sent[i] = nn(w_qb[3 * layer], ups[at(1, layer, b)]).astype(BF)
        regroup_start(i)

    def b3_main(b, layer):
        def step(rows):
            conv_back = cb[b, rows, :]
            extended = jnp.concatenate((conv_back, jnp.zeros((ROWS, LANES), F32)), axis=1)
            signal = us[layer, b, rows, :].astype(F32)
            total = jnp.zeros((ROWS, width), F32)
            for i in range(ntaps):
                tap = jnp.concatenate([tap_of(layer, rows, i)] * (width // LANES), axis=1)
                if i == 0:
                    moved = conv_back
                else:
                    moved = pltpu.roll(extended, width + LANES - i, 1)[:, :width]
                total = total + tap * moved
                term = moved * signal
                narrow = term[:, :LANES]
                for q in range(1, width // LANES):
                    narrow = narrow + term[:, q * LANES : (q + 1) * LANES]
                lanes = slice(i * LANES, (i + 1) * LANES)
                if b > 0:
                    narrow = narrow + tap_acc[rows, lanes]
                tap_acc[rows, lanes] = narrow
            ups[at(2, layer, b), rows, :cut] = total[:, :cut].astype(BF)
            back_tail[b, rows, :] = total[:, cut:]

        in_rows(step)
        i = at(u_b, layer, b)
        upstream = ups[at(2, layer, b), :, :cut]
        sent[i, :, :cut] = nn(w_qb[3 * layer + 1], upstream).astype(BF)

    def b3_edge(b, layer):
        edge_finish(1, layer, b)

        def step(rows):
            after = edge_wide[1, rows, :]
            signal = us[layer, b, rows, cut:].astype(F32)
            total = back_tail[b, rows, :]
            for i in range(1, ntaps):
                moved = jnp.where(lane_of >= LANES - edge, pltpu.roll(after, LANES - i, 1), 0.0)
                total = total + tap_of(layer, rows, i) * moved
                tap_acc[rows, i * LANES : (i + 1) * LANES] += moved * signal
            ups[at(2, layer, b), rows, cut:] = total.astype(BF)

        in_rows(step)
        i = at(u_b, layer, b)
        upstream = ups[at(2, layer, b), :, cut:]
        sent[i, :, cut:] = nn(w_qb[3 * layer + 1], upstream).astype(BF)
        regroup_start(i)

    def b4(b, layer):
        regroup_copy(at(q_b, layer, b)).wait_recv()
        back = nn(w_p[3 * layer], got[at(q_b, layer, b)])
        regroup_copy(at(u_b, layer, b)).wait_recv()
        back = back + nn(w_p[3 * layer + 1], got[at(u_b, layer, b)])
        before = cot[b].astype(F32) if layer == last else flow[b]
        if layer > 0:
            flow[b] = before + back
        else:
            out_x[b] = (before + back).astype(BF)

    def tap_rows(layer):
        total = jnp.zeros((16, tap_width), F32)
        for i in range(ntaps):
            for side in range(2):
                rows = slice(side * tap_width, (side + 1) * tap_width)
                part = tap_acc[rows, i * LANES : (i + 1) * LANES]
                high = part.astype(BF)
                low = (part - high.astype(F32)).astype(BF)
                row = ones_where(e_r == taps_row(layer) + side * ntaps + i)
                total = total + nt(row, high) + nt(row, low)
        if layer == last:
            tap_total[...] = total
        elif layer > 0:
            tap_total[...] += total
        if layer == 1:
            tp_out[0] = tap_total[...].astype(BF)
            taps_start(0)
        if layer == 0:
            tp_out[1] = total.astype(BF)
            taps_start(1)

    both = range(batch)

    def first_term(half, inputs, spread):
        term = nt(inputs[0], spread[0])
        for b in range(1, batch):
            term = term + nt(inputs[b], spread[b])
        return nn(term.astype(BF) * c_mask1[...], c_pack1[half])

    def second_term(half, sections, upstream):
        term = nt(sections[0], upstream[0])
        for b in range(1, batch):
            term = term + nt(sections[b], upstream[b])
        narrow = nn(term.astype(BF) * c_mask2[...], c_pack2[half]).astype(BF)
        return nn(c_permt[...], narrow)

    def every(ref, kind, layer):
        return [ref[at(kind, layer, b)] for b in both]

    def grads_o(layer):
        second_o = second_term(1, every(got, o_f, layer), every(ups, 0, layer))
        first_o = first_term(0, [gs[layer, b] for b in both], every(got, o_b, layer))
        g_out[layer, :, :pair] = (first_o + second_o).astype(BF)

    def grads_second(layer):
        second_q = second_term(0, every(got, q_f, layer), every(ups, 1, layer))
        second_u = second_term(1, every(got, u_f, layer), every(ups, 2, layer))
        g_out[layer, :, pair : 2 * pair] = (second_q + second_u).astype(BF)

    def grads_late(layer):
        inputs = [stream(b, layer) for b in both]
        first_q = first_term(0, inputs, every(got, q_b, layer))
        first_u = first_term(1, inputs, every(got, u_b, layer))
        g_out[layer, :, 2 * pair :] = (first_q + first_u).astype(BF)

    constants_first()
    loads[0].wait()
    make_pt(1)
    make_pt(0)
    loads[1].wait()
    for b in both:
        f1_one(b, 0, 1, u_f)
        f1_one(b, 0, 0, q_f)
    constants_second()
    pl.semaphore_wait(barrier, nh - 1 + parts - 1)
    for b in both:
        regroup_start(at(u_f, 0, b))
        regroup_start(at(q_f, 0, b))
    loads[2].wait()
    make_q(3 * last + 2)
    loads[3].wait()
    for b in both:
        b1(b, last)
    make_q(1)
    make_q(0)
    make_taps(0)
    make_pt(2)
    make_q(2)
    for layer in range(layers):
        if layer == last:
            for m in range(2):
                make_p(3 * last + m)
        for b in both:
            f2_signal(b, layer)
            f2_query(b, layer)
            if layer == last:
                b2_edge(b, layer)
                b3_main(b, layer)
            f3_main(b, layer)
            f3_edge(b, layer)
            if layer < last:
                f3_send(b, layer)
            else:
                b2_query(b, layer)
                b3_edge(b, layer)
        if layer < last:
            for m in range(3):
                make_pt(3 * layer + 3 + m)
            for b in both:
                f4(b, layer)
                f1(b, layer + 1)
            for m in range(3):
                if layer + 1 < last or m < 2:
                    make_q(3 * layer + 3 + m)
            make_taps(layer + 1)
            if layer == 0:
                constants_last()
                make_p(3 * last + 2)
                for b in both:
                    gated_back(b, last)
    for b in both:
        f3_send(b, last)
    for layer in reversed(range(layers)):
        if layer < last:
            for b in both:
                b2_edge(b, layer)
                b2_query(b, layer)
                b3_main(b, layer)
                b3_edge(b, layer)
        tap_rows(layer)
        if layer > 0:
            make_p(3 * layer - 1)
            grads_second(layer)
            if layer < last:
                pair_up(layer + 1)
            for b in both:
                b4(b, layer)
                b1(b, layer - 1)
            if layer == last:
                for b in both:
                    f4(b, last)
            grads_o(layer)
            grads_late(layer)
            pair_copy(layer).start()
            for m in range(2):
                make_p(3 * layer - 3 + m)
            if layer < last:
                total_up(layer + 1)
        else:
            grads_o(0)
            grads_second(0)
            pair_copy(0).start()
            pair_up(1)
            hand_back(2)
            pair_up(0)
    term_q, term_u = None, None
    for b in both:
        regroup_copy(at(q_b, 0, b)).wait_recv()
        more = nt(tok[b], got[at(q_b, 0, b)])
        term_q = more if b == 0 else term_q + more
        if b == batch - 1:
            packed = nn(term_q.astype(BF) * c_mask1[...], c_pack1[0])
        regroup_copy(at(u_b, 0, b)).wait_recv()
        more = nt(tok[b], got[at(u_b, 0, b)])
        term_u = more if b == 0 else term_u + more
    packed = packed + nn(term_u.astype(BF) * c_mask1[...], c_pack1[1])
    g_out[0, :, 2 * pair :] = packed.astype(BF)
    late_scatter()
    for b in both:
        back = nn(w_p[0], got[at(q_b, 0, b)]) + nn(w_p[1], got[at(u_b, 0, b)])
        out_x[b] = (flow[b] + back).astype(BF)
    total_up(1)
    total_up(0)
    taps_total(0)
    taps_total(1)

    for i in range(6 * layers * batch):
        regroup_copy(i).wait_send()
    for layer in range(layers):
        for b in both:
            edge_copy(0, layer, b).wait_send()
            edge_copy(1, layer, b).wait_send()
        pair_copy(layer).wait_send()
        slots_copy(layer).wait_send()
    taps_copy(0).wait_send()
    taps_copy(1).wait_send()
    late_total()
    hand_back(1)
    hand_back(0)
    late_copy(g_out, g_in, 0).wait_send()
    for layer in range(layers):
        parts_copy(layer).wait_send()
        back_copy(layer).wait()
    late_copy(g_sum, g_sum, 1).wait()


def unpack(nb, projections, x, sums, tap, out_x, out_first, out_second, out_taps, held, sems):
    load = pltpu.make_async_copy(sums, held, sems.at[0])
    load.start()
    whole_x = pltpu.make_async_copy(x, out_x, sems.at[1])
    whole_x.start()
    out_taps[...] = tap[...]
    load.wait()
    for layer in range(sums.shape[0]):
        for m in range(projections):
            one = (4 + m if m < 2 else 0) * nb
            two = (2 + m if m < 2 else 1) * nb
            out_first[projections * layer + m] = held[layer, :, one : one + nb]
            out_second[projections * layer + m] = held[layer, :, two : two + nb]
    whole_x.wait()


def body(sizes, tokens, cotangent, first_factors, second_factors, conv_taps):
    nh, nz, ns = sizes
    batch, chan, width = tokens.shape
    layers, ntaps, _ = conv_taps.shape
    nb = first_factors.shape[3]
    projections = first_factors.shape[1]
    parts = nz * ns
    share = chan // parts
    pair = 2 * nb
    many = layers * projections
    dims = (layers, ntaps, batch, chan, width, nb, nh, nz, ns)
    V = pltpu.VMEM
    sq = (chan, chan)
    act = (layers, batch, chan, width)
    regroups = 6 * layers * batch
    grad = (layers, chan, projections * pair)
    scratch = [
        V((chan, nb), BF),
        V((chan, nb), BF),
        V(sq, BF),
        V(sq, BF),
        V(sq, BF),
        V(sq, BF),
        V(sq, BF),
        V(sq, BF),
        V((2, chan, pair), BF),
        V((2, chan, pair), BF),
        V(sq, BF),
        V((many,) + sq, BF),
        V((many,) + sq, BF),
        V((many,) + sq, BF),
        V((many,) + sq, BF),
        V((layers, chan, ntaps * LANES), F32),
        V(act, BF),
        V(act, BF),
        V(act, BF),
        V(act, F32),
        V(act, F32),
        V((3 * layers * batch, chan, width), BF),
        V((batch, chan, width), F32),
        V((batch, chan, width), F32),
        V((regroups, chan, width), BF),
        V((regroups, chan, width), BF),
        V((2 * layers * batch, 16, chan), BF),
        V((2 * layers * batch, 16, chan), BF),
        V((2, chan, LANES), F32),
        V((batch, chan, LANES), F32),
        V((chan, ntaps * LANES), F32),
        V(grad, BF),
        V((layers, nz * share, projections * pair), BF),
        V((layers, nz * share, projections * pair), BF),
        V((layers, parts * share, projections * pair), BF),
        V((2, 16, chan // 2), BF),
        V((2, parts * 16, chan // 2), BF),
        V((16, chan // 2), F32),
        pltpu.SemaphoreType.DMA((regroups,)),
        pltpu.SemaphoreType.DMA((regroups,)),
        pltpu.SemaphoreType.DMA((2 * layers * batch,)),
        pltpu.SemaphoreType.DMA((2 * layers * batch,)),
        pltpu.SemaphoreType.DMA((4 * layers + 4,)),
        pltpu.SemaphoreType.DMA((4 * layers + 4,)),
        V((batch, chan, width), BF),
        V((batch, chan, width), BF),
        V((many, chan, nb), BF),
        V((many, chan, nb), BF),
        pltpu.SemaphoreType.DMA((4,)),
    ]
    whole = pl.BlockSpec(memory_space=pltpu.VMEM)
    anywhere = pl.BlockSpec(memory_space=pl.ANY)
    x_shape = jax.ShapeDtypeStruct((batch, chan, width), BF)
    factor_shape = jax.ShapeDtypeStruct((many, chan, nb), BF)
    taps_shape = jax.ShapeDtypeStruct((layers, ntaps, chan), BF)
    moved = pl.pallas_call(
        functools.partial(kernel, dims),
        out_shape=(x_shape, jax.ShapeDtypeStruct(grad, BF), taps_shape),
        in_specs=[anywhere] * 4 + [whole],
        out_specs=[whole] * 3,
        scratch_shapes=scratch,
        compiler_params=pltpu.CompilerParams(
            collective_id=0, has_side_effects=True, vmem_limit_bytes=56 * 1024 * 1024
        ),
    )(
        tokens,
        cotangent,
        first_factors.reshape(many, chan, nb),
        second_factors.reshape(many, chan, nb),
        conv_taps,
    )
    out_x, out_first, out_second, out_taps = pl.pallas_call(
        functools.partial(unpack, nb, projections),
        out_shape=(x_shape, factor_shape, factor_shape, taps_shape),
        in_specs=[anywhere, anywhere, whole],
        out_specs=[whole] * 4,
        scratch_shapes=[V(grad, BF), pltpu.SemaphoreType.DMA((2,))],
        compiler_params=pltpu.CompilerParams(vmem_limit_bytes=56 * 1024 * 1024),
    )(*moved)
    return (
        out_x,
        out_first.reshape(first_factors.shape),
        out_second.reshape(second_factors.shape),
        out_taps,
    )


def solution(mesh):
    sizes = (mesh.shape["hid"], mesh.shape["dp"], mesh.shape["seq"])
    return jax.shard_map(
        functools.partial(body, sizes),
        mesh=mesh,
        in_specs=(
            P(None, "hid", ("dp", "seq")),
            P(None, "hid", ("dp", "seq")),
            P(None, None, "hid", None, None),
            P(None, None, "hid", None, None),
            P(None, None, "hid"),
        ),
        out_specs=(
            P(None, "hid", ("dp", "seq")),
            P(None, None, "hid", None, None),
            P(None, None, "hid", None, None),
            P(None, None, "hid"),
        ),
        check_vma=False,
    )
```

```python
import functools
import math

import jax
import jax.numpy as jnp
from jax import lax
from jax.experimental import pallas as pl
from jax.experimental.pallas import tpu as pltpu
from jax.sharding import PartitionSpec as P

MESH = pl.DeviceIdType.MESH
BF = jnp.bfloat16
F32 = jnp.float32
LANES = 128
ROWS = 32


def iota(shape, dim):
    return lax.broadcasted_iota(jnp.int32, shape, dim)


def nn(a, b):
    return lax.dot_general(a, b, (((1,), (0,)), ((), ())), preferred_element_type=F32)


def nt(a, b):
    return lax.dot_general(a, b, (((1,), (1,)), ((), ())), preferred_element_type=F32)


def ones_where(condition):
    return jnp.where(condition, 1.0, 0.0).astype(BF)


def kernel(
    dims,
    tok_in,
    cot_in,
    first_in,
    second_in,
    taps,
    out_x,
    g_sum,
    out_taps,
    c_exp1,
    c_exp2,
    c_mask1,
    c_mask1t,
    c_mask2,
    c_mask2t,
    c_perm,
    c_permt,
    c_pack1,
    c_pack2,
    c_same,
    w_p,
    w_pt,
    w_qf,
    w_qb,
    w_taps,
    xs,
    us,
    gs,
    opened,
    convolved,
    ups,
    flow,
    cb,
    sent,
    got,
    edge_out,
    edge_in,
    edge_wide,
    back_tail,
    tap_acc,
    g_out,
    g_pair,
    g_half,
    g_in,
    tp_out,
    tp_in,
    tap_total,
    reg_send,
    reg_recv,
    edge_send,
    edge_recv,
    sum_send,
    sum_recv,
    tok,
    cot,
    first,
    second,
    in_sems,
):
    layers, ntaps, batch, chan, width, nb, nh, nz, ns = dims
    nx = int(math.isqrt(nh))
    ny = nh // nx
    parts = nz * ns
    block = chan // nh
    share = chan // parts
    pair = 2 * nb
    scale = 1.0 / math.sqrt(batch * parts * width)

    me_h = lax.axis_index("hid")
    me_y, me_x = me_h // nx, me_h % nx
    me_z, me_c = lax.axis_index("dp"), lax.axis_index("seq")
    me_p = me_z * ns + me_c

    def far(k, n):
        return min(k, n - k)

    def hid_at(h):
        return (me_z, me_c, h)

    def part_at(p):
        return (p // ns, p % ns, me_h)

    turns = [(dy, dx) for dy in range(ny) for dx in range(nx) if dy + dx > 0]
    turns.sort(key=lambda t: -far(t[0], ny) - far(t[1], nx))
    peers_y = [(me_y + dy) % ny * nx for dy in range(ny)]
    peers_x = [(me_x + dx) % nx for dx in range(nx)]
    hid_peers = [peers_y[dy] + peers_x[dx] for dy, dx in turns]
    steps = sorted(range(1, parts), key=lambda k: -far(k, parts))
    part_peers = [(me_p + k) % parts for k in steps]
    part_ids = [part_at(p) for p in part_peers]

    pairs = ((first_in, first), (tok_in, tok), (second_in, second), (cot_in, cot))
    loads = [pltpu.make_async_copy(a, b, in_sems.at[i]) for i, (a, b) in enumerate(pairs)]
    for load in loads:
        load.start()

    barrier = pltpu.get_barrier_semaphore()

    for h in hid_peers:
        pl.semaphore_signal(barrier, inc=1, device_id=hid_at(h), device_id_type=MESH)
    for where in part_ids:
        pl.semaphore_signal(barrier, inc=1, device_id=where, device_id_type=MESH)

    nb_shift = nb.bit_length() - 1
    r_c, k_c = iota((chan, nb), 0), iota((chan, nb), 1)
    r_s, c_s = iota((chan, chan), 0), iota((chan, chan), 1)
    r_p, k_p = iota((chan, pair), 0), iota((chan, pair), 1)

    def constants_first():
        c_exp1[...] = ones_where(k_c == ((r_c >> 4) << 2) + (r_c & 3))
        c_mask1t[...] = ones_where(((r_s >> 2) & 3) == (c_s >> nb_shift))

    def constants_second():
        c_exp2[...] = ones_where(k_c == (r_c & (nb - 1)))
        c_perm[...] = ones_where(c_s == ((r_s & 3) << nb_shift) + (r_s >> 2))
        c_mask2[...] = ones_where((r_s & 3) == (c_s >> nb_shift))
        c_mask2t[...] = ones_where((c_s & 3) == (r_s >> nb_shift))
        c_same[...] = ones_where(r_s == c_s)

    def constants_last():
        c_mask1[...] = ones_where(((c_s >> 2) & 3) == (r_s >> nb_shift))
        c_permt[...] = ones_where(r_s == ((c_s & 3) << nb_shift) + (c_s >> 2))
        for half in range(2):
            to1 = half * nb + ((r_p >> 4) << 2) + (r_p & 3)
            c_pack1[half] = ones_where(k_p == to1)
            c_pack2[half] = ones_where(k_p == half * nb + (r_p & (nb - 1)))

    def make_pt(i):
        w_pt[i] = nt(c_exp1[...], first[i]).astype(BF) * c_mask1t[...]

    def make_p(i):
        w_p[i] = nt(first[i], c_exp1[...]).astype(BF) * c_mask1[...]

    def make_q(i):
        rows = nn(c_perm[...], second[i]).astype(BF)
        w_qb[i] = nt(rows, c_exp2[...]).astype(BF) * c_mask2[...]
        w_qf[i] = nt(c_exp2[...], rows).astype(BF) * c_mask2t[...]

    def make_taps(layer):
        columns = nt(c_same[...], taps[layer]).astype(BF)
        lane = iota((ntaps, ntaps * LANES), 1) >> 7
        spread = ones_where(lane == iota((ntaps, ntaps * LANES), 0))
        w_taps[layer] = nn(columns, spread)

    own_rows = pl.ds(pl.multiple_of(me_h * block, block), block)

    def at(kind, layer, b):
        return (kind * layers + layer) * batch + b

    def regroup_start(i):
        got[i, own_rows, :] = sent[i, own_rows, :]

        for peer in hid_peers:
            pltpu.make_async_remote_copy(
                src_ref=sent.at[i, pl.ds(pl.multiple_of(peer * block, block), block)],
                dst_ref=got.at[i, own_rows],
                send_sem=reg_send.at[i],
                recv_sem=reg_recv.at[i],
                device_id=hid_at(peer),
                device_id_type=MESH,
            ).start()

    def regroup_copy(i):
        rest = pl.ds(0, (nh - 1) * block)
        return pltpu.make_async_remote_copy(
            src_ref=sent.at[i, rest],
            dst_ref=got.at[i, rest],
            send_sem=reg_send.at[i],
            recv_sem=reg_recv.at[i],
            device_id=hid_at(hid_peers[0]),
            device_id_type=MESH,
        )

    edge = ntaps - 1

    def edge_copy(kind, layer, b):
        i = at(kind, layer, b)
        step = steps.index(1 if kind == 0 else parts - 1)
        return pltpu.make_async_remote_copy(
            src_ref=edge_out.at[i],
            dst_ref=edge_in.at[i],
            send_sem=edge_send.at[i],
            recv_sem=edge_recv.at[i],
            device_id=part_ids[step],
            device_id_type=MESH,
        )

    e_r, e_l = iota((16, LANES), 0), iota((16, LANES), 1)

    def edge_start(kind, layer, b, columns, weight=None):
        lane = e_r + (LANES - edge) if kind == 0 else e_r
        pick = ones_where((e_r < edge) & (e_l == lane))
        rows = nt(pick, columns).astype(BF)
        if weight is not None:
            rows = nt(rows, weight).astype(BF)
        edge_out[at(kind, layer, b)] = rows
        edge_copy(kind, layer, b).start()

    def edge_finish(kind, layer, b):
        edge_copy(kind, layer, b).wait_recv()
        lane = e_r + (LANES - edge) if kind == 0 else e_r
        there = (me_p > 0) if kind == 0 else (me_p < parts - 1)
        keep = jnp.where(there, 1.0, 0.0).astype(F32)
        pick = ones_where((e_r < edge) & (e_l == lane))
        rows = edge_in[at(kind, layer, b)]
        wide = lax.dot_general(rows, pick, (((0,), (0,)), ((), ())), preferred_element_type=F32)
        edge_wide[kind] = wide * keep

    own_share = pl.ds(pl.multiple_of(me_p * share, share), share)
    half = nz * share
    own_half = pl.ds(pl.multiple_of(me_c * half, half), half)
    other_half = pl.ds(pl.multiple_of((ns - 1 - me_c) * half, half), half)
    own_slot = pl.ds(pl.multiple_of(me_z * share, share), share)
    own_part = pl.ds(pl.multiple_of(me_c * half + me_z * share, share), share)
    rest_slots = pl.ds(0, (nz - 1) * share)
    sibling = (me_z, ns - 1 - me_c, me_h)
    steps_z = sorted(range(1, nz), key=lambda k: -far(k, nz))
    peers_z = [(me_z + k) % nz for k in steps_z]
    late = 4 * layers

    def lanes_of(layer):
        return pl.ds(0, (2 if layer == 0 else 3) * pair)

    def sum_copy(sem, source, target, where):
        return pltpu.make_async_remote_copy(
            src_ref=source,
            dst_ref=target,
            send_sem=sum_send.at[sem],
            recv_sem=sum_recv.at[sem],
            device_id=where,
            device_id_type=MESH,
        )

    def pair_copy(layer):
        lanes = lanes_of(layer)
        source = g_out.at[layer, other_half, lanes]
        return sum_copy(4 * layer, source, g_pair.at[layer, pl.ds(0, half), lanes], sibling)

    def slots_copy(layer):
        lanes = lanes_of(layer)
        source = g_half.at[layer, rest_slots, lanes]
        target = g_in.at[layer, rest_slots, lanes]
        return sum_copy(4 * layer + 1, source, target, (peers_z[0], me_c, me_h))

    def parts_copy(layer):
        rows = g_sum.at[layer, rest_slots, lanes_of(layer)]
        return sum_copy(4 * layer + 2, rows, rows, (peers_z[0], me_c, me_h))

    def back_copy(layer):
        rows = g_sum.at[layer, own_half, lanes_of(layer)]
        return sum_copy(4 * layer + 3, rows, rows, sibling)

    def pair_up(layer):
        pair_copy(layer).wait_recv()
        lanes = lanes_of(layer)
        total = g_out[layer, own_half, lanes].astype(F32)
        total = total + g_pair[layer, pl.ds(0, half), lanes].astype(F32)
        g_half[layer, pl.ds(0, half), lanes] = total.astype(BF)
        g_in[layer, own_slot, lanes] = g_half[layer, own_slot, lanes]
        for z in peers_z:
            away = pl.ds(pl.multiple_of(z * share, share), share)
            source = g_half.at[layer, away, lanes]
            target = g_in.at[layer, own_slot, lanes]
            sum_copy(4 * layer + 1, source, target, (z, me_c, me_h)).start()

    def total_up(layer):
        slots_copy(layer).wait_recv()
        lanes = lanes_of(layer)
        total = g_in[layer, pl.ds(0, share), lanes].astype(F32)
        for z in range(1, nz):
            total = total + g_in[layer, pl.ds(z * share, share), lanes].astype(F32)
        g_sum[layer, own_part, lanes] = (total * scale).astype(BF)
        rows = g_sum.at[layer, own_part, lanes]
        for z in peers_z:
            sum_copy(4 * layer + 2, rows, rows, (z, me_c, me_h)).start()

    def hand_back(layer):
        parts_copy(layer).wait_recv()
        back_copy(layer).start()

    late_lanes = pl.ds(2 * pair, pair)

    def late_copy(source, target, back):
        rest = pl.ds(0, (parts - 1) * share)
        one, two = source.at[0, rest, late_lanes], target.at[0, rest, late_lanes]
        return sum_copy(late + back, one, two, part_ids[0])

    def late_scatter():
        g_in[0, own_share, late_lanes] = g_out[0, own_share, late_lanes]
        target = g_in.at[0, own_share, late_lanes]
        for peer, where in zip(part_peers, part_ids):
            away = pl.ds(pl.multiple_of(peer * share, share), share)
            sum_copy(late, g_out.at[0, away, late_lanes], target, where).start()

    def late_total():
        late_copy(g_out, g_in, 0).wait_recv()
        total = g_in[0, pl.ds(0, share), late_lanes].astype(F32)
        for p in range(1, parts):
            total = total + g_in[0, pl.ds(p * share, share), late_lanes].astype(F32)
        g_sum[0, own_share, late_lanes] = (total * scale).astype(BF)
        rows = g_sum.at[0, own_share, late_lanes]
        for where in part_ids:
            sum_copy(late + 1, rows, rows, where).start()

    def taps_start(tile):
        own = pl.ds(pl.multiple_of(me_p * 16, 16), 16)
        tp_in[tile, own, :] = tp_out[tile]
        for where in part_ids:
            sum_copy(late + 2 + tile, tp_out.at[tile], tp_in.at[tile, own], where).start()

    def taps_copy(tile):
        rest = tp_in.at[tile, pl.ds(0, (parts - 1) * 16)]
        return sum_copy(late + 2 + tile, rest, rest, part_ids[0])

    def taps_total(tile):
        taps_copy(tile).wait_recv()
        total = tp_in[tile, pl.ds(0, 16), :].astype(F32)
        for p in range(1, parts):
            total = total + tp_in[tile, pl.ds(p * 16, 16), :].astype(F32)
        total = (total * scale).astype(BF)
        for layer in range(layers):
            if (layer == 0) == (tile == 1):
                for side in range(2):
                    row = taps_row(layer) + side * ntaps
                    lanes = slice(side * tap_width, (side + 1) * tap_width)
                    out_taps[layer, :, lanes] = total[row : row + ntaps, :]

    tap_width = chan // 2

    def taps_row(layer):
        return 0 if layer == 0 else (layers - 1 - layer) * 2 * ntaps

    def in_rows(step):
        def one(r, _):
            step(pl.ds(pl.multiple_of(r * ROWS, ROWS), ROWS))
            return 0

        lax.fori_loop(0, chan // ROWS, one, 0, unroll=True)

    u_f, q_f, o_f, o_b, q_b, u_b = range(6)
    last = layers - 1
    cut = width - LANES

    def stream(b, layer):
        return tok[b] if layer == 0 else xs[layer, b]

    def f1_one(b, layer, m, kind):
        sent[at(kind, layer, b)] = nn(w_pt[3 * layer + m], stream(b, layer)).astype(BF)

    def f1(b, layer):
        for m, kind in ((1, u_f), (0, q_f)):
            f1_one(b, layer, m, kind)
            regroup_start(at(kind, layer, b))

    def f2_signal(b, layer):
        i = at(u_f, layer, b)
        regroup_copy(i).wait_recv()
        edge_start(0, layer, b, got[i, :, cut:], w_qf[3 * layer + 1])
        us[layer, b] = nn(w_qf[3 * layer + 1], got[i]).astype(BF)

    def f2_query(b, layer):
        i = at(q_f, layer, b)
        regroup_copy(i).wait_recv()
        query = nn(w_qf[3 * layer], got[i]).astype(BF).astype(F32)
        opened[layer, b] = jax.nn.sigmoid(query)

    def tap_of(layer, rows, i):
        return w_taps[layer, rows, i * LANES : (i + 1) * LANES]

    lane_of = iota((ROWS, LANES), 1)

    def f3_main(b, layer):
        def step(rows):
            signal = us[layer, b, rows, :].astype(F32)
            extended = jnp.concatenate((jnp.zeros((ROWS, LANES), F32), signal), axis=1)
            total = jnp.zeros((ROWS, width), F32)
            for i in range(ntaps):
                tap = jnp.concatenate([tap_of(layer, rows, i)] * (width // LANES), axis=1)
                moved = signal if i == 0 else pltpu.roll(extended, i, 1)[:, LANES:]
                total = total + tap * moved
            convolved[layer, b, rows, :] = total
            gated = opened[layer, b, rows, LANES:] * total[:, LANES:]
            gs[layer, b, rows, LANES:] = gated.astype(BF)

        in_rows(step)
        if layer < last:
            i = at(o_f, layer, b)
            sent[i, :, LANES:] = nn(w_pt[3 * layer + 2], gs[layer, b, :, LANES:]).astype(BF)

    def f3_edge(b, layer):
        edge_finish(0, layer, b)

        def step(rows):
            before = edge_wide[0, rows, :]
            more = jnp.zeros((ROWS, LANES), F32)
            for i in range(1, ntaps):
                more = more + tap_of(layer, rows, i) * pltpu.roll(before, i, 1)
            total = convolved[layer, b, rows, :LANES] + jnp.where(lane_of < edge, more, 0.0)
            convolved[layer, b, rows, :LANES] = total
            gs[layer, b, rows, :LANES] = (opened[layer, b, rows, :LANES] * total).astype(BF)

        in_rows(step)

    def f3_send(b, layer):
        i = at(o_f, layer, b)
        if layer < last:
            sent[i, :, :LANES] = nn(w_pt[3 * layer + 2], gs[layer, b, :, :LANES]).astype(BF)
        else:
            sent[i] = nn(w_pt[3 * layer + 2], gs[layer, b]).astype(BF)
        regroup_start(i)

    def f4(b, layer):
        i = at(o_f, layer, b)
        regroup_copy(i).wait_recv()
        if layer < last:
            branch = nn(w_qf[3 * layer + 2], got[i])
            xs[layer + 1, b] = (stream(b, layer).astype(F32) + branch).astype(BF)

    def b1_spread(b, layer):
        upstream = cot[b] if layer == last else flow[b].astype(BF)
        ups[at(0, layer, b)] = upstream
        sent[at(o_b, layer, b)] = nn(w_qb[3 * layer + 2], upstream).astype(BF)

    def b1(b, layer):
        b1_spread(b, layer)
        regroup_start(at(o_b, layer, b))

    def gated_back(b, layer):
        i = at(o_b, layer, b)
        regroup_copy(i).wait_recv()
        cb[b] = nn(w_p[3 * layer + 2], got[i])

    def b2_edge(b, layer):
        if layer < last:
            i = at(o_b, layer, b)
            regroup_copy(i).wait_recv()
            head = nn(w_p[3 * layer + 2], got[i, :, :LANES])
        else:
            head = cb[b, :, :LANES]
        head = head * opened[layer, b, :, :LANES]
        edge_start(1, layer, b, head.astype(BF))
        cb[b, :, :LANES] = head
        if layer < last:
            rest = nn(w_p[3 * layer + 2], got[i, :, LANES:])
        else:
            rest = cb[b, :, LANES:]
        cb[b, :, LANES:] = rest * opened[layer, b, :, LANES:]

    def b2_query(b, layer):
        def step(rows):
            shut = 1.0 - opened[layer, b, rows, :]
            back = cb[b, rows, :] * convolved[layer, b, rows, :] * shut
            ups[at(1, layer, b), rows, :] = back.astype(BF)

        in_rows(step)
        i = at(q_b, layer, b)
        sent[i] = nn(w_qb[3 * layer], ups[at(1, layer, b)]).astype(BF)
        regroup_start(i)

    def b3_main(b, layer):
        def step(rows):
            conv_back = cb[b, rows, :]
            extended = jnp.concatenate((conv_back, jnp.zeros((ROWS, LANES), F32)), axis=1)
            signal = us[layer, b, rows, :].astype(F32)
            total = jnp.zeros((ROWS, width), F32)
            for i in range(ntaps):
                tap = jnp.concatenate([tap_of(layer, rows, i)] * (width // LANES), axis=1)
                if i == 0:
                    moved = conv_back
                else:
                    moved = pltpu.roll(extended, width + LANES - i, 1)[:, :width]
                total = total + tap * moved
                term = moved * signal
                narrow = term[:, :LANES]
                for q in range(1, width // LANES):
                    narrow = narrow + term[:, q * LANES : (q + 1) * LANES]
                lanes = slice(i * LANES, (i + 1) * LANES)
                if b > 0:
                    narrow = narrow + tap_acc[rows, lanes]
                tap_acc[rows, lanes] = narrow
            ups[at(2, layer, b), rows, :cut] = total[:, :cut].astype(BF)
            back_tail[b, rows, :] = total[:, cut:]

        in_rows(step)
        i = at(u_b, layer, b)
        upstream = ups[at(2, layer, b), :, :cut]
        sent[i, :, :cut] = nn(w_qb[3 * layer + 1], upstream).astype(BF)

    def b3_edge(b, layer):
        edge_finish(1, layer, b)

        def step(rows):
            after = edge_wide[1, rows, :]
            signal = us[layer, b, rows, cut:].astype(F32)
            total = back_tail[b, rows, :]
            for i in range(1, ntaps):
                moved = jnp.where(lane_of >= LANES - edge, pltpu.roll(after, LANES - i, 1), 0.0)
                total = total + tap_of(layer, rows, i) * moved
                tap_acc[rows, i * LANES : (i + 1) * LANES] += moved * signal
            ups[at(2, layer, b), rows, cut:] = total.astype(BF)

        in_rows(step)
        i = at(u_b, layer, b)
        upstream = ups[at(2, layer, b), :, cut:]
        sent[i, :, cut:] = nn(w_qb[3 * layer + 1], upstream).astype(BF)
        regroup_start(i)

    def b4(b, layer):
        regroup_copy(at(q_b, layer, b)).wait_recv()
        back = nn(w_p[3 * layer], got[at(q_b, layer, b)])
        regroup_copy(at(u_b, layer, b)).wait_recv()
        back = back + nn(w_p[3 * layer + 1], got[at(u_b, layer, b)])
        before = cot[b].astype(F32) if layer == last else flow[b]
        if layer > 0:
            flow[b] = before + back
        else:
            out_x[b] = (before + back).astype(BF)

    def tap_rows(layer):
        total = jnp.zeros((16, tap_width), F32)
        for i in range(ntaps):
            for side in range(2):
                rows = slice(side * tap_width, (side + 1) * tap_width)
                part = tap_acc[rows, i * LANES : (i + 1) * LANES]
                high = part.astype(BF)
                low = (part - high.astype(F32)).astype(BF)
                row = ones_where(e_r == taps_row(layer) + side * ntaps + i)
                total = total + nt(row, high) + nt(row, low)
        if layer == last:
            tap_total[...] = total
        elif layer > 0:
            tap_total[...] += total
        if layer == 1:
            tp_out[0] = tap_total[...].astype(BF)
            taps_start(0)
        if layer == 0:
            tp_out[1] = total.astype(BF)
            taps_start(1)

    both = range(batch)

    def first_term(half, inputs, spread):
        term = nt(inputs[0], spread[0])
        for b in range(1, batch):
            term = term + nt(inputs[b], spread[b])
        return nn(term.astype(BF) * c_mask1[...], c_pack1[half])

    def second_term(half, sections, upstream):
        term = nt(sections[0], upstream[0])
        for b in range(1, batch):
            term = term + nt(sections[b], upstream[b])
        narrow = nn(term.astype(BF) * c_mask2[...], c_pack2[half]).astype(BF)
        return nn(c_permt[...], narrow)

    def every(ref, kind, layer):
        return [ref[at(kind, layer, b)] for b in both]

    def grads_o(layer):
        second_o = second_term(1, every(got, o_f, layer), every(ups, 0, layer))
        first_o = first_term(0, [gs[layer, b] for b in both], every(got, o_b, layer))
        g_out[layer, :, :pair] = (first_o + second_o).astype(BF)

    def grads_second(layer):
        second_q = second_term(0, every(got, q_f, layer), every(ups, 1, layer))
        second_u = second_term(1, every(got, u_f, layer), every(ups, 2, layer))
        g_out[layer, :, pair : 2 * pair] = (second_q + second_u).astype(BF)

    def grads_late(layer):
        inputs = [stream(b, layer) for b in both]
        first_q = first_term(0, inputs, every(got, q_b, layer))
        first_u = first_term(1, inputs, every(got, u_b, layer))
        g_out[layer, :, 2 * pair :] = (first_q + first_u).astype(BF)

    constants_first()
    loads[0].wait()
    make_pt(1)
    make_pt(0)
    loads[1].wait()
    for b in both:
        f1_one(b, 0, 1, u_f)
        f1_one(b, 0, 0, q_f)
    constants_second()
    pl.semaphore_wait(barrier, nh - 1 + parts - 1)
    for kind in (u_f, q_f):
        for b in both:
            regroup_start(at(kind, 0, b))
    loads[2].wait()
    make_q(3 * last + 2)
    loads[3].wait()
    for b in both:
        b1(b, last)
    make_q(1)
    make_q(0)
    make_taps(0)
    make_pt(2)
    make_q(2)
    for layer in range(layers):
        if layer == last:
            for m in range(2):
                make_p(3 * last + m)
        for b in both:
            f2_signal(b, layer)
            f2_query(b, layer)
            if layer == last:
                b2_edge(b, layer)
                b3_main(b, layer)
            f3_main(b, layer)
            f3_edge(b, layer)
            if layer < last:
                f3_send(b, layer)
            else:
                b2_query(b, layer)
                b3_edge(b, layer)
        if layer < last:
            for m in range(3):
                make_pt(3 * layer + 3 + m)
            for b in both:
                f4(b, layer)
                f1(b, layer + 1)
            for m in range(3):
                if layer + 1 < last or m < 2:
                    make_q(3 * layer + 3 + m)
            make_taps(layer + 1)
            if layer == 0:
                constants_last()
                make_p(3 * last + 2)
                for b in both:
                    gated_back(b, last)
    for b in both:
        f3_send(b, last)
    for layer in reversed(range(layers)):
        if layer < last:
            for b in both:
                b2_edge(b, layer)
                b2_query(b, layer)
                b3_main(b, layer)
                b3_edge(b, layer)
        tap_rows(layer)
        if layer > 0:
            make_p(3 * layer - 1)
            grads_second(layer)
            if layer < last:
                pair_up(layer + 1)
            for b in both:
                b4(b, layer)
                b1(b, layer - 1)
            if layer == last:
                for b in both:
                    f4(b, last)
            grads_o(layer)
            grads_late(layer)
            pair_copy(layer).start()
            for m in range(2):
                make_p(3 * layer - 3 + m)
            if layer < last:
                total_up(layer + 1)
        else:
            grads_o(0)
            grads_second(0)
            pair_copy(0).start()
            pair_up(1)
            hand_back(2)
            pair_up(0)
    term_q, term_u = None, None
    for b in both:
        regroup_copy(at(q_b, 0, b)).wait_recv()
        more = nt(tok[b], got[at(q_b, 0, b)])
        term_q = more if b == 0 else term_q + more
        if b == batch - 1:
            packed = nn(term_q.astype(BF) * c_mask1[...], c_pack1[0])
        regroup_copy(at(u_b, 0, b)).wait_recv()
        more = nt(tok[b], got[at(u_b, 0, b)])
        term_u = more if b == 0 else term_u + more
    packed = packed + nn(term_u.astype(BF) * c_mask1[...], c_pack1[1])
    g_out[0, :, 2 * pair :] = packed.astype(BF)
    late_scatter()
    for b in both:
        back = nn(w_p[0], got[at(q_b, 0, b)]) + nn(w_p[1], got[at(u_b, 0, b)])
        out_x[b] = (flow[b] + back).astype(BF)
    total_up(1)
    total_up(0)
    taps_total(0)
    taps_total(1)

    for i in range(6 * layers * batch):
        regroup_copy(i).wait_send()
    for layer in range(layers):
        for b in both:
            edge_copy(0, layer, b).wait_send()
            edge_copy(1, layer, b).wait_send()
        pair_copy(layer).wait_send()
        slots_copy(layer).wait_send()
    taps_copy(0).wait_send()
    taps_copy(1).wait_send()
    late_total()
    hand_back(1)
    hand_back(0)
    late_copy(g_out, g_in, 0).wait_send()
    for layer in range(layers):
        parts_copy(layer).wait_send()
        back_copy(layer).wait()
    late_copy(g_sum, g_sum, 1).wait()


def unpack(nb, projections, x, sums, tap, out_x, out_first, out_second, out_taps, held, sems):
    load = pltpu.make_async_copy(sums, held, sems.at[0])
    load.start()
    whole_x = pltpu.make_async_copy(x, out_x, sems.at[1])
    whole_x.start()
    out_taps[...] = tap[...]
    load.wait()
    for layer in range(sums.shape[0]):
        for m in range(projections):
            one = (4 + m if m < 2 else 0) * nb
            two = (2 + m if m < 2 else 1) * nb
            out_first[projections * layer + m] = held[layer, :, one : one + nb]
            out_second[projections * layer + m] = held[layer, :, two : two + nb]
    whole_x.wait()


def body(sizes, tokens, cotangent, first_factors, second_factors, conv_taps):
    nh, nz, ns = sizes
    batch, chan, width = tokens.shape
    layers, ntaps, _ = conv_taps.shape
    nb = first_factors.shape[3]
    projections = first_factors.shape[1]
    parts = nz * ns
    share = chan // parts
    pair = 2 * nb
    many = layers * projections
    dims = (layers, ntaps, batch, chan, width, nb, nh, nz, ns)
    V = pltpu.VMEM
    sq = (chan, chan)
    act = (layers, batch, chan, width)
    regroups = 6 * layers * batch
    grad = (layers, chan, projections * pair)
    scratch = [
        V((chan, nb), BF),
        V((chan, nb), BF),
        V(sq, BF),
        V(sq, BF),
        V(sq, BF),
        V(sq, BF),
        V(sq, BF),
        V(sq, BF),
        V((2, chan, pair), BF),
        V((2, chan, pair), BF),
        V(sq, BF),
        V((many,) + sq, BF),
        V((many,) + sq, BF),
        V((many,) + sq, BF),
        V((many,) + sq, BF),
        V((layers, chan, ntaps * LANES), F32),
        V(act, BF),
        V(act, BF),
        V(act, BF),
        V(act, F32),
        V(act, F32),
        V((3 * layers * batch, chan, width), BF),
        V((batch, chan, width), F32),
        V((batch, chan, width), F32),
        V((regroups, chan, width), BF),
        V((regroups, chan, width), BF),
        V((2 * layers * batch, 16, chan), BF),
        V((2 * layers * batch, 16, chan), BF),
        V((2, chan, LANES), F32),
        V((batch, chan, LANES), F32),
        V((chan, ntaps * LANES), F32),
        V(grad, BF),
        V((layers, nz * share, projections * pair), BF),
        V((layers, nz * share, projections * pair), BF),
        V((layers, parts * share, projections * pair), BF),
        V((2, 16, chan // 2), BF),
        V((2, parts * 16, chan // 2), BF),
        V((16, chan // 2), F32),
        pltpu.SemaphoreType.DMA((regroups,)),
        pltpu.SemaphoreType.DMA((regroups,)),
        pltpu.SemaphoreType.DMA((2 * layers * batch,)),
        pltpu.SemaphoreType.DMA((2 * layers * batch,)),
        pltpu.SemaphoreType.DMA((4 * layers + 4,)),
        pltpu.SemaphoreType.DMA((4 * layers + 4,)),
        V((batch, chan, width), BF),
        V((batch, chan, width), BF),
        V((many, chan, nb), BF),
        V((many, chan, nb), BF),
        pltpu.SemaphoreType.DMA((4,)),
    ]
    whole = pl.BlockSpec(memory_space=pltpu.VMEM)
    anywhere = pl.BlockSpec(memory_space=pl.ANY)
    x_shape = jax.ShapeDtypeStruct((batch, chan, width), BF)
    factor_shape = jax.ShapeDtypeStruct((many, chan, nb), BF)
    taps_shape = jax.ShapeDtypeStruct((layers, ntaps, chan), BF)
    moved = pl.pallas_call(
        functools.partial(kernel, dims),
        out_shape=(x_shape, jax.ShapeDtypeStruct(grad, BF), taps_shape),
        in_specs=[anywhere] * 4 + [whole],
        out_specs=[whole] * 3,
        scratch_shapes=scratch,
        compiler_params=pltpu.CompilerParams(
            collective_id=0, has_side_effects=True, vmem_limit_bytes=56 * 1024 * 1024
        ),
    )(
        tokens,
        cotangent,
        first_factors.reshape(many, chan, nb),
        second_factors.reshape(many, chan, nb),
        conv_taps,
    )
    out_x, out_first, out_second, out_taps = pl.pallas_call(
        functools.partial(unpack, nb, projections),
        out_shape=(x_shape, factor_shape, factor_shape, taps_shape),
        in_specs=[anywhere, anywhere, whole],
        out_specs=[whole] * 4,
        scratch_shapes=[V(grad, BF), pltpu.SemaphoreType.DMA((2,))],
        compiler_params=pltpu.CompilerParams(vmem_limit_bytes=56 * 1024 * 1024),
    )(*moved)
    return (
        out_x,
        out_first.reshape(first_factors.shape),
        out_second.reshape(second_factors.shape),
        out_taps,
    )


def solution(mesh):
    sizes = (mesh.shape["hid"], mesh.shape["dp"], mesh.shape["seq"])
    return jax.shard_map(
        functools.partial(body, sizes),
        mesh=mesh,
        in_specs=(
            P(None, "hid", ("dp", "seq")),
            P(None, "hid", ("dp", "seq")),
            P(None, None, "hid", None, None),
            P(None, None, "hid", None, None),
            P(None, None, "hid"),
        ),
        out_specs=(
            P(None, "hid", ("dp", "seq")),
            P(None, None, "hid", None, None),
            P(None, None, "hid", None, None),
            P(None, None, "hid"),
        ),
        check_vma=False,
    )
```
